128 devices in a mesh: dp: 8 (over x, y_lo), owner: 16 (over y_hi, z, core).
Axes of the slice: x: 4, y: 4 (y_hi: 2, y_lo: 2; y = y_hi * 2 + y_lo), z: 4, core: 2. Of those that a mesh axis runs over, the one named last changes fastest.
Arguments:
- grad_partials: bfloat16 [8, 128, 512, 512], P('dp', 'owner'), may hold values from -2.5 to 2.5
- owner_slot: int32 [16, 8], replicated, may hold values from 0 to 7, each once within a row
- refresh_blocks: int32 [32], replicated, may hold values from 0 to 127, as said below
- left_stat: float32 [16, 8, 512, 512], P('owner', 'dp'), as said below
- right_stat: float32 [16, 8, 512, 512], P('owner', 'dp'), as said below
- left_root: bfloat16 [16, 8, 512, 512], P('owner', 'dp'), as said below
- right_root: bfloat16 [16, 8, 512, 512], P('owner', 'dp'), as said below
Outputs:
- update: bfloat16 [16, 8, 512, 512], P(None, 'dp')
- left_stat_new: float32 [16, 8, 512, 512], P('owner', 'dp')
- right_stat_new: float32 [16, 8, 512, 512], P('owner', 'dp')
- left_root_new: bfloat16 [16, 8, 512, 512], P('owner', 'dp')
- right_root_new: bfloat16 [16, 8, 512, 512], P('owner', 'dp')
The draws below stay inside these ranges and needn't reach their ends.
Inputs may be any that keep to these rules, and one draw needn't show every extreme that they name: `owner_slot`: each row is an ordering of the 8 slots of one owner group. `refresh_blocks`: 32 distinct block numbers, always including block 0 and block 127. `left_stat`: each block is symmetric positive definite. `right_stat`: each block is symmetric positive definite. `left_root`: each block is symmetric. `right_root`: each block is symmetric.
All inputs are finite; a program needn't handle non-finite values.
Results may differ from the reference program's by a relative error of at most 0.02.
Values may be sent and summed in bfloat16 or wider, within the bound.
A program may use at most 128 MiB of HBM per device.

```python
import jax
import jax.numpy as jnp
from jax import lax

ORDER = 512
ITERS = 4
SLOTS = 8
BLOCKS = 128
REFRESH = 32
N_DP = 8
N_OWNER = 16


def blockwise_sym(key, shape, diag_lo, diag_hi):
    key_diag = jax.random.fold_in(key, 0)
    key_norm = jax.random.fold_in(key, 2)
    size = shape[-1]
    diag_vals = jnp.exp(jax.random.uniform(key_diag, shape[:-1], jnp.float32, jnp.log(diag_lo), jnp.log(diag_hi)))
    raw_normal = jnp.clip(jax.random.normal(key_norm, shape, jnp.float32), -2.5, 2.5)
    noise = raw_normal
    symmetric = (noise + jnp.swapaxes(noise, -1, -2)) * 0.70710678
    off_scale = 0.25 / jnp.sqrt(jnp.float32(size))
    outer_scale = jnp.sqrt(diag_vals[..., :, None] * diag_vals[..., None, :])
    identity_mat = jnp.eye(size, dtype=jnp.float32)
    return symmetric * off_scale * outer_scale * (1.0 - identity_mat) + diag_vals[..., None] * identity_mat


def draw_refresh_blocks(key, part):
    key = jax.random.fold_in(key, 5)
    key_pick, key_order = jax.random.split(key)
    middle = jax.random.permutation(key_pick, BLOCKS - 2)[:REFRESH - 2].astype(jnp.int32) + 1
    ends = jnp.array([0, BLOCKS - 1], dtype=jnp.int32)
    chosen = jnp.concatenate([ends, middle])
    shuffle = jax.random.permutation(key_order, REFRESH)
    return chosen[shuffle].astype(jnp.int32)


def draw_left_stat(key, part):
    key = jax.random.fold_in(key, 11)
    shape = (N_OWNER, SLOTS, ORDER, ORDER)
    return blockwise_sym(key, shape, 1.0, 10.0)


def draw_right_stat(key, part):
    key = jax.random.fold_in(key, 13)
    shape = (N_OWNER, SLOTS, ORDER, ORDER)
    return blockwise_sym(key, shape, 1.0, 10.0)


def draw_left_root(key, part):
    key = jax.random.fold_in(key, 17)
    shape = (N_OWNER, SLOTS, ORDER, ORDER)
    return blockwise_sym(key, shape, 0.5, 1.0).astype(jnp.bfloat16)


def draw_right_root(key, part):
    key = jax.random.fold_in(key, 19)
    shape = (N_OWNER, SLOTS, ORDER, ORDER)
    return blockwise_sym(key, shape, 0.5, 1.0).astype(jnp.bfloat16)


def levels(key, shape, shards, least, largest):
    level, own = 1.0, jax.random.fold_in(key, 6)
    for dim, blocks in shards:
        steps = jnp.exp(jax.random.uniform(jax.random.fold_in(own, dim), (blocks,), jnp.float32, least / len(shards), largest / len(shards)))
        level = level * jnp.repeat(steps, shape[dim] // blocks).reshape([-1 if axis == dim else 1 for axis in range(len(shape))])
    return level


def gaussian(rng, dims, width, most, pieces=(), kind=jnp.bfloat16):
    entries = jax.random.normal(rng, dims, jnp.float32) * width
    if len(pieces) > 0:
        entries = levels(rng, dims, pieces, -0.22, 0.18) * entries
    return jnp.clip(entries, min=-most, max=most).astype(kind)


def setup_inputs(seed: int = 0) -> dict:
    streams_of = jax.random.split(jax.random.key(seed), 8)
    return {
        "grad_partials": gaussian(streams_of[0], (N_DP, BLOCKS, ORDER, ORDER), 0.35, 2.5, ((0, 8), (1, 16))),
        "owner_slot": jax.vmap(lambda own: jax.random.permutation(own, SLOTS))(jax.random.split(streams_of[1], N_OWNER)).reshape((N_OWNER, SLOTS)).astype(jnp.int32),
        "refresh_blocks": draw_refresh_blocks(jax.random.fold_in(streams_of[7], 71), 0),
        "left_stat": draw_left_stat(jax.random.fold_in(streams_of[7], 71), 0),
        "right_stat": draw_right_stat(jax.random.fold_in(streams_of[7], 71), 0),
        "left_root": draw_left_root(jax.random.fold_in(streams_of[7], 71), 0),
        "right_root": draw_right_root(jax.random.fold_in(streams_of[7], 71), 0),
    }


decay_rate = 0.8
graft_eps = 1e-06
full_prec = lax.Precision.HIGHEST

def inverse_root(stacked):
    size = stacked.shape[-1]
    identity_mat = jnp.eye(size, dtype=jnp.float32)
    scale = 2.0 * jnp.trace(stacked, axis1=1, axis2=2) / size
    scaled = stacked / scale[:, None, None]
    root = identity_mat[None] * (scale ** (-0.25))[:, None, None]
    for sweep_index in range(ITERS):
        factor = (5.0 * identity_mat - scaled) * 0.25
        squared = jnp.einsum('kab,kbc->kac', factor, factor, precision=full_prec)
        fourth = jnp.einsum('kab,kbc->kac', squared, squared, precision=full_prec)
        scaled = jnp.einsum('kab,kbc->kac', fourth, scaled, precision=full_prec)
        root = jnp.einsum('kab,kbc->kac', root, factor, precision=full_prec)
    return root

def reference(grad_partials, owner_slot, refresh_blocks, left_stat, right_stat, left_root, right_root):
    size = ORDER
    grad = grad_partials[0].astype(jnp.float32)
    for replica in range(1, N_DP):
        grad = grad + grad_partials[replica].astype(jnp.float32)
    order_index = jnp.argsort(owner_slot, axis=1).astype(jnp.int32)
    group_base = jnp.arange(N_OWNER, dtype=jnp.int32)[:, None] * SLOTS
    block_of_slot = (group_base + order_index).reshape(-1)
    grad_slot = grad[block_of_slot]
    stat_weight = (1.0 - decay_rate) / size
    left_flat = left_stat.reshape(BLOCKS, size, size)
    right_flat = right_stat.reshape(BLOCKS, size, size)
    left_new = decay_rate * left_flat + stat_weight * jnp.einsum('kab,kcb->kac', grad_slot, grad_slot, precision=full_prec)
    right_new = decay_rate * right_flat + stat_weight * jnp.einsum('kba,kbc->kac', grad_slot, grad_slot, precision=full_prec)
    slot_of_block = (group_base + owner_slot).reshape(-1).astype(jnp.int32)
    positions = slot_of_block[refresh_blocks].astype(jnp.int32)

    def refresh_one(where_at):
        pair = jnp.stack([left_new[where_at], right_new[where_at]])
        return inverse_root(pair).astype(jnp.bfloat16)
    fresh = lax.map(refresh_one, positions)
    left_roots = left_root.reshape(BLOCKS, size, size).at[positions].set(fresh[:, 0])
    right_roots = right_root.reshape(BLOCKS, size, size).at[positions].set(fresh[:, 1])
    grad_low = grad_slot.astype(jnp.bfloat16)
    left_part = jnp.einsum('kab,kbc->kac', left_roots.astype(jnp.float32), grad_low.astype(jnp.float32), precision=full_prec).astype(jnp.bfloat16)
    raw = jnp.einsum('kab,kbc->kac', left_part.astype(jnp.float32), right_roots.astype(jnp.float32), precision=full_prec)
    graft = jnp.sqrt(lax.optimization_barrier(jnp.mean(grad_slot * grad_slot, axis=(1, 2)))) / jnp.sqrt(lax.optimization_barrier(jnp.mean(raw * raw, axis=(1, 2))) + graft_eps)
    update = (raw * graft[:, None, None]).astype(jnp.bfloat16)
    shape_out = (N_OWNER, SLOTS, size, size)
    return (update.reshape(shape_out), left_new.reshape(shape_out), right_new.reshape(shape_out), left_roots.reshape(shape_out), right_roots.reshape(shape_out))
```

```python
import jax
import jax.numpy as jnp
from jax import lax
from jax.experimental import pallas as pl
from jax.experimental.pallas import tpu as pltpu
from jax.sharding import PartitionSpec as P

MESH = pl.DeviceIdType.MESH
f32 = jnp.float32
bf16 = jnp.bfloat16

N = 512
XS, ZS, SLOTS, REFRESH = 4, 4, 8, 32
decay_rate = 0.8
graft_eps = 1e-06

RA, RAH = 288, 144
RB, RBH = N - RA, (N - RA) // 2
A_LO, A_HI, A_ALL = pl.ds(0, RAH), pl.ds(RAH, RAH), pl.ds(0, RA)
B_LO, B_HI, B_ALL = pl.ds(RA, RBH), pl.ds(RA + RBH, RBH), pl.ds(RA, RB)
LO_A, HI_A = pl.ds(0, RAH), pl.ds(RAH, RAH)
LO_B, HI_B = pl.ds(0, RBH), pl.ds(RBH, RBH)


def position():
    dp, ow = lax.axis_index("dp"), lax.axis_index("owner")
    return dp // 2, dp % 2, ow // 8, (ow // 2) % 4, ow % 2


def greet(targets):
    barrier = pltpu.get_barrier_semaphore()
    for target in targets:
        pl.semaphore_signal(barrier, inc=1, device_id=target, device_id_type=MESH)
    pl.semaphore_wait(barrier, len(targets))


class Copies:
    def __init__(self, send_sem, recv_sem):
        self.send_sem, self.recv_sem, self.started = send_sem, recv_sem, {}

    def start(self, name, src, dst, target):
        at = len(self.started)
        copy = pltpu.make_async_remote_copy(
            src_ref=src, dst_ref=dst, send_sem=self.send_sem.at[at], recv_sem=self.recv_sem.at[at],
            device_id=target, device_id_type=MESH)
        copy.start()
        self.started[name] = copy

    def arrived(self, *names):
        for name in names:
            self.started[name].wait_recv()

    def finish(self):
        for copy in self.started.values():
            copy.wait_send()


def reduce_kernel(owner_slot, partials, g_ref, st, ra1, ra2, ra3, rb1, sb, rb2, rb3, acc_a, acc_b, sum_a, send_sem, recv_sem):
    x, yl, yh, z, c = position()
    dp, ow = lax.axis_index("dp"), lax.axis_index("owner")
    xp = (((x + 1) % XS) * 2 + yl, ow)
    xm = (((x + XS - 1) % XS) * 2 + yl, ow)
    yo = (x * 2 + 1 - yl, ow)
    greet((xp, xm, yo))
    go = Copies(send_sem, recv_sem)

    def block_of(dx, dy):
        slot = ((x + dx) % XS) * 2 + (yl + dy) % 2
        found = jnp.int32(0)
        for r in range(SLOTS):
            found = jnp.where(owner_slot[ow, r] == slot, jnp.int32(r), found)
        return found

    where = {(dx, dy): block_of(dx, dy) for dx in range(XS) for dy in range(2)}

    def stage(dx, dy, rows):
        st[dx * 2 + dy, rows, :] = partials[where[dx, dy], rows, :]

    def own(dx, dy, rows):
        return st.at[dx * 2 + dy, rows]

    def first_a(dy):
        stage(2, dy, A_ALL)
        go.start(("a1p", dy), own(2, dy, A_LO), ra1.at[0, dy], xp)
        go.start(("a1m", dy), own(2, dy, A_HI), ra1.at[1, dy], xm)

    def own_a(dy):
        stage(1, dy, A_ALL)
        go.start(("a2p", dy), own(1, dy, A_HI), ra2.at[0, dy, HI_A], xp)
        stage(3, dy, A_ALL)
        go.start(("a2m", dy), own(3, dy, A_LO), ra2.at[1, dy, LO_A], xm)

    def sum_of_a(dy):
        go.arrived(("a1p", dy), ("a1m", dy))
        acc_a[0, dy] = (st[2 + dy, A_LO, :].astype(f32) + ra1[0, dy].astype(f32)).astype(bf16)
        go.start(("a3p", dy), acc_a.at[0, dy], ra2.at[0, dy, LO_A], xp)
        acc_a[1, dy] = (st[6 + dy, A_HI, :].astype(f32) + ra1[1, dy].astype(f32)).astype(bf16)
        go.start(("a3m", dy), acc_a.at[1, dy], ra2.at[1, dy, HI_A], xm)

    def first_b(dx):
        stage(dx, 1, B_ALL)
        go.start(("b1", dx), own(dx, 1, B_ALL), rb1.at[dx], yo)

    def sum_of_b(dx):
        stage(dx, 0, B_ALL)
        go.arrived(("b1", dx))
        sb[dx] = (st[dx * 2, B_ALL, :].astype(f32) + rb1[dx].astype(f32)).astype(bf16)

    first_a(1)
    first_b(2)
    first_a(0)
    own_a(1)
    first_b(1)
    stage(0, 0, A_ALL)
    stage(0, 1, A_ALL)
    sum_of_a(1)
    sum_of_b(2)
    first_b(3)
    own_a(0)
    sum_of_a(0)
    go.start("b2p", sb.at[2, LO_B], rb2.at[0], xp)
    go.start("b2m", sb.at[2, HI_B], rb2.at[1], xm)
    sum_of_b(1)
    first_b(0)
    go.start("b3p", sb.at[1, HI_B], rb3.at[0, HI_B], xp)
    go.arrived(("a2p", 1), ("a2m", 1), ("a3p", 1), ("a3m", 1))
    sum_a[...] = (st[1, A_ALL, :].astype(f32) + ra2[0, 1].astype(f32) + ra2[1, 1].astype(f32)).astype(bf16)
    go.start("a4", sum_a, ra3, yo)
    sum_of_b(3)
    go.start("b3m", sb.at[3, LO_B], rb3.at[1, LO_B], xm)
    go.arrived("b2p", "b2m")
    acc_b[0] = (sb[1, LO_B, :].astype(f32) + rb2[0].astype(f32)).astype(bf16)
    go.start("b4p", acc_b.at[0], rb3.at[0, LO_B], xp)
    acc_b[1] = (sb[3, HI_B, :].astype(f32) + rb2[1].astype(f32)).astype(bf16)
    go.start("b4m", acc_b.at[1], rb3.at[1, HI_B], xm)
    go.arrived(("a2p", 0), ("a2m", 0), ("a3p", 0), ("a3m", 0))
    stage(0, 0, B_ALL)
    go.arrived(("b1", 0))
    go.arrived("a4")
    g_ref[A_ALL, :] = (st[0, A_ALL, :].astype(f32) + ra2[0, 0].astype(f32) + ra2[1, 0].astype(f32)
                       + ra3[...].astype(f32)).astype(bf16)
    go.arrived("b3p", "b3m", "b4p", "b4m")
    g_ref[B_ALL, :] = (st[0, B_ALL, :].astype(f32) + rb1[0].astype(f32) + rb3[0].astype(f32)
                       + rb3[1].astype(f32)).astype(bf16)
    go.finish()


def reduce_scatter(owner_slot, partials):
    vm = lambda *shape: pltpu.VMEM(shape + (N,), bf16)
    return pl.pallas_call(
        reduce_kernel,
        out_shape=jax.ShapeDtypeStruct((N, N), bf16),
        in_specs=[pl.BlockSpec(memory_space=pltpu.SMEM), pl.BlockSpec(memory_space=pltpu.VMEM)],
        out_specs=pl.BlockSpec(memory_space=pltpu.VMEM),
        scratch_shapes=[
            vm(SLOTS, N), vm(2, 2, RAH), vm(2, 2, RA), vm(RA), vm(XS, RB), vm(XS, RB), vm(2, RBH), vm(2, RB),
            vm(2, 2, RAH), vm(2, RBH), vm(RA),
            pltpu.SemaphoreType.DMA((23,)), pltpu.SemaphoreType.DMA((23,)),
        ],
        compiler_params=pltpu.CompilerParams(collective_id=0, has_side_effects=True, vmem_limit_bytes=40 * 2**20),
        name="reduce_scatter",
    )(owner_slot, partials)


def dot(a, b):
    return jnp.dot(a, b, preferred_element_type=f32)


def split(a):
    high = a.astype(bf16)
    return high, (a - high.astype(f32)).astype(bf16)


def total(a):
    return jnp.sum(jnp.sum(a, axis=0, keepdims=True), axis=1, keepdims=True)


def root(stat):
    rows = lax.broadcasted_iota(jnp.int32, (N, N), 0)
    cols = lax.broadcasted_iota(jnp.int32, (N, N), 1)
    eye = jnp.where(rows == cols, 1.0, 0.0).astype(f32)
    scale = total(stat * eye) * (2.0 / N)
    d = (eye - stat * (1.0 / scale)) * 0.25
    h = eye + d
    dh, dl = split(d)
    d2 = dot(dh, dh) + (dot(dh, dl) + dot(dl, dh))
    d2h, d2l = split(d2)
    d3 = dot(dh, d2h) + (dot(dh, d2l) + dot(dl, d2h))
    uh, ul = split(3.75 * d2 + d3)
    d = 2.5 * d2 + 5.0 * d3 + (dot(d2h, uh) + (dot(d2h, ul) + dot(d2l, uh)))
    for sweep in range(3):
        low = d.astype(bf16)
        h = h + dot(h.astype(bf16), low)
        if sweep == 2:
            break
        d2 = dot(low, low)
        d2h = d2.astype(bf16)
        d3 = dot(low, d2h)
        d = 2.5 * d2 + 5.0 * d3 + dot(d2h, (3.75 * d2 + d3).astype(bf16))
    return h * lax.rsqrt(jnp.sqrt(scale))


def local_kernel(owner_slot, refresh, g_ref, left_stat, right_stat, left_root, right_root,
                 update, left_new, right_new, left_out, right_out):
    dp, ow = lax.axis_index("dp"), lax.axis_index("owner")
    block = ow * SLOTS
    for r in range(SLOTS):
        block = block + jnp.where(owner_slot[ow, r] == dp, jnp.int32(r), jnp.int32(0))
    hits = jnp.int32(0)
    for i in range(REFRESH):
        hits = hits + jnp.where(refresh[i] == block, jnp.int32(1), jnp.int32(0))
    g = g_ref[...]
    gt = g.T
    weight = (1.0 - decay_rate) / N
    left_new[...] = decay_rate * left_stat[...] + weight * dot(g, gt)
    right_new[...] = decay_rate * right_stat[...] + weight * dot(gt, g)

    @pl.when(hits > 0)
    def _():
        left_out[...] = root(left_new[...]).astype(bf16)
        right_out[...] = root(right_new[...]).astype(bf16)

    @pl.when(hits == 0)
    def _():
        left_out[...] = left_root[...]
        right_out[...] = right_root[...]

    raw = dot(dot(left_out[...], g).astype(bf16), right_out[...])
    gf = g.astype(f32)
    graft = jnp.sqrt(total(gf * gf) * (1.0 / (N * N))) / jnp.sqrt(total(raw * raw) * (1.0 / (N * N)) + graft_eps)
    update[...] = (raw * graft).astype(bf16)


def local_step(owner_slot, refresh, g, left_stat, right_stat, left_root, right_root):
    vmem, smem = pl.BlockSpec(memory_space=pltpu.VMEM), pl.BlockSpec(memory_space=pltpu.SMEM)
    like = lambda dtype: jax.ShapeDtypeStruct((N, N), dtype)
    return pl.pallas_call(
        local_kernel,
        out_shape=(like(bf16), like(f32), like(f32), like(bf16), like(bf16)),
        in_specs=[smem] * 2 + [vmem] * 5,
        out_specs=[vmem] * 5,
        compiler_params=pltpu.CompilerParams(vmem_limit_bytes=40 * 2**20),
        name="local_step",
    )(owner_slot, refresh, g, left_stat, right_stat, left_root, right_root)


RY, RYH = 288, 144
RZ, RZH = N - RY, (N - RY) // 2
Y_ALL, Y_LO, Y_HI = pl.ds(0, RY), pl.ds(0, RYH), pl.ds(RYH, RYH)
Z_ALL, Z_LO, Z_HI = pl.ds(RY, RZ), pl.ds(RY, RZH), pl.ds(RY + RZH, RZH)


def gather_kernel(update, out, send_sem, recv_sem):
    x, yl, yh, z, c = position()
    dp, ow = lax.axis_index("dp"), lax.axis_index("owner")

    def owner(dz, dy, dc=0):
        return (((yh + dy) % 2) * ZS + (z + dz) % ZS) * 2 + (c + dc) % 2

    zp, zm = (dp, owner(1, 0)), (dp, owner(3, 0))
    yo, co = (dp, owner(0, 1)), (dp, owner(0, 0, 1))
    greet((zp, zm, yo, co))
    go = Copies(send_sem, recv_sem)

    def pass_on(name, dz, dy, rows, target):
        piece = out.at[owner(dz, dy), rows]
        go.start(name, piece, piece, target)

    def share(dz, dy, rows, tag):
        pass_on(("core", dz, dy, tag), dz, dy, rows, co)

    def mine(name, rows, target):
        go.start(name, update.at[rows], out.at[owner(0, 0), rows], target)

    mine("yY", Y_ALL, yo)
    mine("zZ+", Z_ALL, zp)
    mine("zZ-", Z_ALL, zm)
    mine("zY+", Y_ALL, zp)
    mine("zY-", Y_ALL, zm)
    mine("yZ", Z_ALL, yo)
    mine("core", pl.ds(0, N), co)
    out[owner(0, 0)] = update[...]

    go.arrived("zZ+")
    pass_on("zZ2+", 3, 0, Z_LO, zp)
    pass_on("yZ-", 3, 0, Z_ALL, yo)
    share(3, 0, Z_ALL, "Z")
    go.arrived("zZ-")
    pass_on("zZ2-", 1, 0, Z_HI, zm)
    pass_on("yZ+", 1, 0, Z_ALL, yo)
    share(1, 0, Z_ALL, "Z")
    go.arrived("yY")
    pass_on("pY+", 0, 1, Y_ALL, zp)
    pass_on("pY-", 0, 1, Y_ALL, zm)
    share(0, 1, Y_ALL, "Y")
    go.arrived("zY+")
    pass_on("zY2+", 3, 0, Y_LO, zp)
    share(3, 0, Y_ALL, "Y")
    go.arrived("zY-")
    pass_on("zY2-", 1, 0, Y_HI, zm)
    share(1, 0, Y_ALL, "Y")
    go.arrived("yZ")
    share(0, 1, Z_ALL, "Z")
    go.arrived("zZ2+", "zZ2-")
    pass_on("yZ2", 2, 0, Z_ALL, yo)
    share(2, 0, Z_ALL, "Z")
    go.arrived("yZ-")
    share(3, 1, Z_ALL, "Z")
    go.arrived("pY+")
    pass_on("pY2+", 3, 1, Y_LO, zp)
    share(3, 1, Y_ALL, "Y")
    go.arrived("pY-")
    pass_on("pY2-", 1, 1, Y_HI, zm)
    share(1, 1, Y_ALL, "Y")
    go.arrived("yZ+")
    share(1, 1, Z_ALL, "Z")
    go.arrived("zY2+", "zY2-")
    share(2, 0, Y_ALL, "Y")
    go.arrived("yZ2")
    share(2, 1, Z_ALL, "Z")
    go.arrived("pY2+", "pY2-")
    share(2, 1, Y_ALL, "Y")
    go.arrived("core", *[name for name in go.started if name[0] == "core" and len(name) == 4 and name != "core"])
    go.finish()


def all_gather(update):
    copies = 12 + 6 + 15
    return pl.pallas_call(
        gather_kernel,
        out_shape=jax.ShapeDtypeStruct((16, N, N), bf16),
        in_specs=[pl.BlockSpec(memory_space=pltpu.VMEM)],
        out_specs=pl.BlockSpec(memory_space=pltpu.VMEM),
        scratch_shapes=[pltpu.SemaphoreType.DMA((copies,)), pltpu.SemaphoreType.DMA((copies,))],
        compiler_params=pltpu.CompilerParams(collective_id=1, has_side_effects=True, vmem_limit_bytes=40 * 2**20),
        name="all_gather",
    )(update)


def body(grad_partials, owner_slot, refresh_blocks, left_stat, right_stat, left_root, right_root):
    g = reduce_scatter(owner_slot, grad_partials[0])
    update, left_new, right_new, left_out, right_out = local_step(
        owner_slot, refresh_blocks, g, left_stat[0, 0], right_stat[0, 0], left_root[0, 0], right_root[0, 0])
    gathered = all_gather(update)
    return (gathered[:, None], left_new[None, None], right_new[None, None], left_out[None, None], right_out[None, None])


def solution(mesh):
    slots = P("owner", "dp", None, None)
    return jax.shard_map(
        body,
        mesh=mesh,
        in_specs=(P("dp", "owner", None, None), P(), P(), slots, slots, slots, slots),
        out_specs=(P(None, "dp", None, None), slots, slots, slots, slots),
        check_vma=False,
    )
```

```python
import jax
import jax.numpy as jnp
from jax import lax
from jax.experimental import pallas as pl
from jax.experimental.pallas import tpu as pltpu
from jax.sharding import PartitionSpec as P

MESH = pl.DeviceIdType.MESH
f32 = jnp.float32
bf16 = jnp.bfloat16

N = 512
XS, ZS, SLOTS, REFRESH = 4, 4, 8, 32
decay_rate = 0.8
graft_eps = 1e-06

RA, RAH = 288, 144
RB, RBH = N - RA, (N - RA) // 2
A_LO, A_HI, A_ALL = pl.ds(0, RAH), pl.ds(RAH, RAH), pl.ds(0, RA)
B_LO, B_HI, B_ALL = pl.ds(RA, RBH), pl.ds(RA + RBH, RBH), pl.ds(RA, RB)
LO_A, HI_A = pl.ds(0, RAH), pl.ds(RAH, RAH)
LO_B, HI_B = pl.ds(0, RBH), pl.ds(RBH, RBH)


def position():
    dp, ow = lax.axis_index("dp"), lax.axis_index("owner")
    return dp // 2, dp % 2, ow // 8, (ow // 2) % 4, ow % 2


def greet(targets):
    barrier = pltpu.get_barrier_semaphore()
    for target in targets:
        pl.semaphore_signal(barrier, inc=1, device_id=target, device_id_type=MESH)
    pl.semaphore_wait(barrier, len(targets))


class Copies:
    def __init__(self, send_sem, recv_sem):
        self.send_sem, self.recv_sem, self.started = send_sem, recv_sem, {}

    def start(self, name, src, dst, target):
        at = len(self.started)
        copy = pltpu.make_async_remote_copy(
            src_ref=src, dst_ref=dst, send_sem=self.send_sem.at[at], recv_sem=self.recv_sem.at[at],
            device_id=target, device_id_type=MESH)
        copy.start()
        self.started[name] = copy

    def arrived(self, *names):
        for name in names:
            self.started[name].wait_recv()

    def finish(self):
        for copy in self.started.values():
            copy.wait_send()


RY, RYH = 288, 144
RZ, RZH = N - RY, (N - RY) // 2
Y_ALL, Y_LO, Y_HI = pl.ds(0, RY), pl.ds(0, RYH), pl.ds(RYH, RYH)
Z_ALL, Z_LO, Z_HI = pl.ds(RY, RZ), pl.ds(RY, RZH), pl.ds(RY + RZH, RZH)


def dot(a, b):
    return jnp.dot(a, b, preferred_element_type=f32)


def split(a):
    high = a.astype(bf16)
    return high, (a - high.astype(f32)).astype(bf16)


def total(a):
    return jnp.sum(jnp.sum(a, axis=0, keepdims=True), axis=1, keepdims=True)


def root(stat):
    rows = lax.broadcasted_iota(jnp.int32, (N, N), 0)
    cols = lax.broadcasted_iota(jnp.int32, (N, N), 1)
    eye = jnp.where(rows == cols, 1.0, 0.0).astype(f32)
    scale = total(stat * eye) * (2.0 / N)
    d = (eye - stat * (1.0 / scale)) * 0.25
    h = eye + d
    dh, dl = split(d)
    d2 = dot(dh, dh) + (dot(dh, dl) + dot(dl, dh))
    d2h, d2l = split(d2)
    d3 = dot(dh, d2h) + (dot(dh, d2l) + dot(dl, d2h))
    uh, ul = split(3.75 * d2 + d3)
    d = 2.5 * d2 + 5.0 * d3 + (dot(d2h, uh) + (dot(d2h, ul) + dot(d2l, uh)))
    for sweep in range(3):
        low = d.astype(bf16)
        h = h + dot(h.astype(bf16), low)
        if sweep == 2:
            break
        d2 = dot(low, low)
        d2h = d2.astype(bf16)
        d3 = dot(low, d2h)
        d = 2.5 * d2 + 5.0 * d3 + dot(d2h, (3.75 * d2 + d3).astype(bf16))
    return h * lax.rsqrt(jnp.sqrt(scale))


def step_kernel(owner_slot, refresh, partials_hbm, left_stat_hbm, right_stat_hbm, left_root_hbm, right_root_hbm,
                out, left_new, right_new, left_out, right_out,
                partials, left_stat, right_stat, left_root, right_root, g, update,
                st, ra1, ra2, ra3, rb1, sb, rb2, rb3, acc_a, acc_b, sum_a, send_sem, recv_sem, load_sem):
    loads = [pltpu.make_async_copy(partials_hbm.at[i], partials.at[i], load_sem.at[i]) for i in range(SLOTS)]
    stats = [pltpu.make_async_copy(src, dst, load_sem.at[SLOTS + i]) for i, (src, dst) in enumerate((
        (left_stat_hbm, left_stat), (right_stat_hbm, right_stat), (left_root_hbm, left_root), (right_root_hbm, right_root)))]
    for copy in loads:
        copy.start()
    x, yl, yh, z, c = position()
    dp, ow = lax.axis_index("dp"), lax.axis_index("owner")

    def owner(dz, dy, dc=0):
        return (((yh + dy) % 2) * ZS + (z + dz) % ZS) * 2 + (c + dc) % 2

    xp = (((x + 1) % XS) * 2 + yl, ow)
    xm = (((x + XS - 1) % XS) * 2 + yl, ow)
    yo = (x * 2 + 1 - yl, ow)
    zp, zm = (dp, owner(1, 0)), (dp, owner(3, 0))
    yp, co = (dp, owner(0, 1)), (dp, owner(0, 0, 1))
    greet((xp, xm, yo, zp, zm, yp, co))
    for copy in loads:
        copy.wait()
    go = Copies(send_sem, recv_sem)

    def block_of(dx, dy):
        slot = ((x + dx) % XS) * 2 + (yl + dy) % 2
        found = jnp.int32(0)
        for r in range(SLOTS):
            found = jnp.where(owner_slot[ow, r] == slot, jnp.int32(r), found)
        return found

    where = {(dx, dy): block_of(dx, dy) for dx in range(XS) for dy in range(2)}

    def stage(dx, dy, rows):
        st[dx * 2 + dy, rows, :] = partials[where[dx, dy], rows, :]

    def own(dx, dy, rows):
        return st.at[dx * 2 + dy, rows]

    def first_a(dy):
        stage(2, dy, A_ALL)
        go.start(("a1p", dy), own(2, dy, A_LO), ra1.at[0, dy], xp)
        go.start(("a1m", dy), own(2, dy, A_HI), ra1.at[1, dy], xm)

    def own_a(dy):
        stage(1, dy, A_ALL)
        go.start(("a2p", dy), own(1, dy, A_HI), ra2.at[0, dy, HI_A], xp)
        stage(3, dy, A_ALL)
        go.start(("a2m", dy), own(3, dy, A_LO), ra2.at[1, dy, LO_A], xm)

    def sum_of_a(dy):
        go.arrived(("a1p", dy), ("a1m", dy))
        acc_a[0, dy] = (st[2 + dy, A_LO, :].astype(f32) + ra1[0, dy].astype(f32)).astype(bf16)
        go.start(("a3p", dy), acc_a.at[0, dy], ra2.at[0, dy, LO_A], xp)
        acc_a[1, dy] = (st[6 + dy, A_HI, :].astype(f32) + ra1[1, dy].astype(f32)).astype(bf16)
        go.start(("a3m", dy), acc_a.at[1, dy], ra2.at[1, dy, HI_A], xm)

    def first_b(dx):
        stage(dx, 1, B_ALL)
        go.start(("b1", dx), own(dx, 1, B_ALL), rb1.at[dx], yo)

    def sum_of_b(dx):
        stage(dx, 0, B_ALL)
        go.arrived(("b1", dx))
        sb[dx] = (st[dx * 2, B_ALL, :].astype(f32) + rb1[dx].astype(f32)).astype(bf16)

    first_a(1)
    for copy in stats:
        copy.start()
    first_b(2)
    first_a(0)
    own_a(1)
    first_b(1)
    stage(0, 0, A_ALL)
    stage(0, 1, A_ALL)
    sum_of_a(1)
    sum_of_b(2)
    first_b(3)
    own_a(0)
    sum_of_a(0)
    go.start("b2p", sb.at[2, LO_B], rb2.at[0], xp)
    go.start("b2m", sb.at[2, HI_B], rb2.at[1], xm)
    sum_of_b(1)
    first_b(0)
    go.start("b3p", sb.at[1, HI_B], rb3.at[0, HI_B], xp)
    go.arrived(("a2p", 1), ("a2m", 1), ("a3p", 1), ("a3m", 1))
    sum_a[...] = (st[1, A_ALL, :].astype(f32) + ra2[0, 1].astype(f32) + ra2[1, 1].astype(f32)).astype(bf16)
    go.start("a4", sum_a, ra3, yo)
    sum_of_b(3)
    go.start("b3m", sb.at[3, LO_B], rb3.at[1, LO_B], xm)
    go.arrived("b2p", "b2m")
    acc_b[0] = (sb[1, LO_B, :].astype(f32) + rb2[0].astype(f32)).astype(bf16)
    go.start("b4p", acc_b.at[0], rb3.at[0, LO_B], xp)
    acc_b[1] = (sb[3, HI_B, :].astype(f32) + rb2[1].astype(f32)).astype(bf16)
    go.start("b4m", acc_b.at[1], rb3.at[1, HI_B], xm)
    go.arrived(("a2p", 0), ("a2m", 0), ("a3p", 0), ("a3m", 0))
    stage(0, 0, B_ALL)
    go.arrived(("b1", 0))
    go.arrived("a4")
    g[A_ALL, :] = (st[0, A_ALL, :].astype(f32) + ra2[0, 0].astype(f32) + ra2[1, 0].astype(f32)
                       + ra3[...].astype(f32)).astype(bf16)
    go.arrived("b3p", "b3m", "b4p", "b4m")
    g[B_ALL, :] = (st[0, B_ALL, :].astype(f32) + rb1[0].astype(f32) + rb3[0].astype(f32)
                       + rb3[1].astype(f32)).astype(bf16)

    block = ow * SLOTS
    for r in range(SLOTS):
        block = jnp.where(owner_slot[ow, r] == dp, ow * SLOTS + r, block)
    hits = jnp.int32(0)
    for i in range(REFRESH):
        hits = hits + jnp.where(refresh[i] == block, jnp.int32(1), jnp.int32(0))
    for copy in stats:
        copy.wait()
    low = g[...]
    low_t = low.T
    weight = (1.0 - decay_rate) / N
    left_new[...] = decay_rate * left_stat[...] + weight * dot(low, low_t)
    right_new[...] = decay_rate * right_stat[...] + weight * dot(low_t, low)
    left_out[...] = jnp.where(hits > 0, root(left_new[...]), left_root[...].astype(f32)).astype(bf16)
    right_out[...] = jnp.where(hits > 0, root(right_new[...]), right_root[...].astype(f32)).astype(bf16)
    raw = dot(dot(left_out[...], low).astype(bf16), right_out[...])
    full = low.astype(f32)
    graft = jnp.sqrt(total(full * full) * (1.0 / (N * N))) / jnp.sqrt(total(raw * raw) * (1.0 / (N * N)) + graft_eps)
    update[...] = (raw * graft).astype(bf16)

    def pass_on(name, dz, dy, rows, target):
        piece = out.at[owner(dz, dy), rows]
        go.start(name, piece, piece, target)

    def share(dz, dy, rows, tag):
        pass_on(("core", dz, dy, tag), dz, dy, rows, co)

    def mine(name, rows, target):
        go.start(name, update.at[rows], out.at[owner(0, 0), rows], target)

    mine("yY", Y_ALL, yp)
    mine("zZ+", Z_ALL, zp)
    mine("zZ-", Z_ALL, zm)
    mine("zY+", Y_ALL, zp)
    mine("zY-", Y_ALL, zm)
    mine("yZ", Z_ALL, yp)
    mine("core", pl.ds(0, N), co)
    out[owner(0, 0)] = update[...]

    go.arrived("zZ+")
    pass_on("zZ2+", 3, 0, Z_LO, zp)
    pass_on("yZ-", 3, 0, Z_ALL, yp)
    share(3, 0, Z_ALL, "Z")
    go.arrived("zZ-")
    pass_on("zZ2-", 1, 0, Z_HI, zm)
    pass_on("yZ+", 1, 0, Z_ALL, yp)
    share(1, 0, Z_ALL, "Z")
    go.arrived("yY")
    pass_on("pY+", 0, 1, Y_ALL, zp)
    pass_on("pY-", 0, 1, Y_ALL, zm)
    share(0, 1, Y_ALL, "Y")
    go.arrived("zY+")
    pass_on("zY2+", 3, 0, Y_LO, zp)
    share(3, 0, Y_ALL, "Y")
    go.arrived("zY-")
    pass_on("zY2-", 1, 0, Y_HI, zm)
    share(1, 0, Y_ALL, "Y")
    go.arrived("yZ")
    share(0, 1, Z_ALL, "Z")
    go.arrived("zZ2+", "zZ2-")
    pass_on("yZ2", 2, 0, Z_ALL, yp)
    share(2, 0, Z_ALL, "Z")
    go.arrived("yZ-")
    share(3, 1, Z_ALL, "Z")
    go.arrived("pY+")
    pass_on("pY2+", 3, 1, Y_LO, zp)
    share(3, 1, Y_ALL, "Y")
    go.arrived("pY-")
    pass_on("pY2-", 1, 1, Y_HI, zm)
    share(1, 1, Y_ALL, "Y")
    go.arrived("yZ+")
    share(1, 1, Z_ALL, "Z")
    go.arrived("zY2+", "zY2-")
    share(2, 0, Y_ALL, "Y")
    go.arrived("yZ2")
    share(2, 1, Z_ALL, "Z")
    go.arrived("pY2+", "pY2-")
    share(2, 1, Y_ALL, "Y")
    go.arrived("core", *[name for name in go.started if name[0] == "core" and len(name) == 4 and name != "core"])
    go.finish()


def whole_step(*arrays):
    vmem, smem, hbm = (pl.BlockSpec(memory_space=space) for space in (pltpu.VMEM, pltpu.SMEM, pltpu.HBM))
    like = lambda dtype, *lead: pltpu.VMEM(lead + (N, N), dtype)
    vm = lambda *shape: pltpu.VMEM(shape + (N,), bf16)
    copies = 23 + 33
    return pl.pallas_call(
        step_kernel,
        out_shape=(like(bf16, 16), like(f32), like(f32), like(bf16), like(bf16)),
        in_specs=[smem] * 2 + [hbm] * 5,
        out_specs=[vmem] * 5,
        scratch_shapes=[
            vm(SLOTS, N), pltpu.VMEM((N, N), f32), pltpu.VMEM((N, N), f32), vm(N), vm(N), vm(N), vm(N),
            vm(SLOTS, N), vm(2, 2, RAH), vm(2, 2, RA), vm(RA), vm(XS, RB), vm(XS, RB), vm(2, RBH), vm(2, RB),
            vm(2, 2, RAH), vm(2, RBH), vm(RA),
            pltpu.SemaphoreType.DMA((copies,)), pltpu.SemaphoreType.DMA((copies,)), pltpu.SemaphoreType.DMA((SLOTS + 4,)),
        ],
        compiler_params=pltpu.CompilerParams(collective_id=0, has_side_effects=True, vmem_limit_bytes=44 * 2**20),
        name="whole_step",
    )(*arrays)


def write_kernel(*refs):
    count = len(refs) // 2
    sems = refs[-1]
    copies, at = [], 0
    for src, dst in zip(refs[:count], refs[count:-1]):
        parts = [(src.at[i], dst.at[i]) for i in range(src.shape[0])] if len(src.shape) == 3 else [(src, dst)]
        for part in parts:
            copies.append(pltpu.make_async_copy(*part, sems.at[at]))
            copies[-1].start()
            at += 1
    for copy in copies:
        copy.wait()


def write_out(arrays):
    return pl.pallas_call(
        write_kernel,
        out_shape=tuple(jax.ShapeDtypeStruct(a.shape, a.dtype) for a in arrays),
        in_specs=[pl.BlockSpec(memory_space=pltpu.VMEM)] * len(arrays),
        out_specs=[pl.BlockSpec(memory_space=pl.ANY)] * len(arrays),
        scratch_shapes=[pltpu.SemaphoreType.DMA((20,))],
        compiler_params=pltpu.CompilerParams(vmem_limit_bytes=2**20),
        name="write_out",
    )(*arrays)


def body(grad_partials, owner_slot, refresh_blocks, left_stat, right_stat, left_root, right_root):
    results = whole_step(owner_slot, refresh_blocks, grad_partials[0], left_stat[0, 0], right_stat[0, 0], left_root[0, 0], right_root[0, 0])
    update, *own = write_out(results)
    return (update[:, None], *(array[None, None] for array in own))


def solution(mesh):
    slots = P("owner", "dp", None, None)
    return jax.shard_map(
        body,
        mesh=mesh,
        in_specs=(P("dp", "owner", None, None), P(), P(), slots, slots, slots, slots),
        out_specs=(P(None, "dp", None, None), slots, slots, slots, slots),
        check_vma=False,
    )
```

```python
import jax
import jax.numpy as jnp
from jax import lax
from jax.experimental import pallas as pl
from jax.experimental.pallas import tpu as pltpu
from jax.sharding import PartitionSpec as P

MESH = pl.DeviceIdType.MESH
f32 = jnp.float32
bf16 = jnp.bfloat16

N = 512
XS, ZS, SLOTS, REFRESH = 4, 4, 8, 32
ITERS = 4
decay_rate = 0.8
graft_eps = 1e-06

RA, RAH = 288, 144
RB, RBH = N - RA, (N - RA) // 2
A_LO, A_HI, A_ALL = pl.ds(0, RAH), pl.ds(RAH, RAH), pl.ds(0, RA)
B_LO, B_HI, B_ALL = pl.ds(RA, RBH), pl.ds(RA + RBH, RBH), pl.ds(RA, RB)
LO_A, HI_A = pl.ds(0, RAH), pl.ds(RAH, RAH)
LO_B, HI_B = pl.ds(0, RBH), pl.ds(RBH, RBH)


def position():
    dp, ow = lax.axis_index("dp"), lax.axis_index("owner")
    return dp // 2, dp % 2, ow // 8, (ow // 2) % 4, ow % 2


def greet(targets):
    barrier = pltpu.get_barrier_semaphore()
    for target in targets:
        pl.semaphore_signal(barrier, inc=1, device_id=target, device_id_type=MESH)
    pl.semaphore_wait(barrier, len(targets))


class Copies:
    def __init__(self, send_sem, recv_sem):
        self.send_sem, self.recv_sem, self.started = send_sem, recv_sem, {}

    def start(self, name, src, dst, target):
        at = len(self.started)
        copy = pltpu.make_async_remote_copy(
            src_ref=src, dst_ref=dst, send_sem=self.send_sem.at[at], recv_sem=self.recv_sem.at[at],
            device_id=target, device_id_type=MESH)
        copy.start()
        self.started[name] = copy

    def arrived(self, *names):
        for name in names:
            self.started[name].wait_recv()

    def finish(self):
        for copy in self.started.values():
            copy.wait_send()


RY, RYH = 288, 144
RZ, RZH = N - RY, (N - RY) // 2
Y_ALL, Y_LO, Y_HI = pl.ds(0, RY), pl.ds(0, RYH), pl.ds(RYH, RYH)
Z_ALL, Z_LO, Z_HI = pl.ds(RY, RZ), pl.ds(RY, RZH), pl.ds(RY + RZH, RZH)


def dot(a, b):
    return jnp.dot(a, b, preferred_element_type=f32)


def split(a):
    high = a.astype(bf16)
    return high, (a - high.astype(f32)).astype(bf16)


def total(a):
    return jnp.sum(jnp.sum(a, axis=0, keepdims=True), axis=1, keepdims=True)


def roots(stats, keep, kept, outs, d, q, u, hb, h, w, wide, tall):
    rows = lax.broadcasted_iota(jnp.int32, (N, N), 0)
    cols = lax.broadcasted_iota(jnp.int32, (N, N), 1)
    both = range(2)
    final = []
    for m in both:
        eye = jnp.where(rows == cols, 1.0, 0.0).astype(f32)
        stat = stats[m][...]
        scale = total(stat * eye) * (2.0 / N)
        final.append(lax.rsqrt(jnp.sqrt(scale)))
        first = (eye - stat * (1.0 / scale)) * 0.25
        high, rest = split(first)
        d[m] = high
        h[m] = eye + first
        hb[m] = (eye + first).astype(bf16)
        wide[m, :, 0:N], wide[m, :, N:2 * N], wide[m, :, 2 * N:3 * N] = high, high, rest
        tall[m, 0:N, :], tall[m, N:2 * N, :], tall[m, 2 * N:3 * N, :] = high, rest, high
    for sweep in range(ITERS):
        for m in both:
            if sweep > 0:
                new = h[m] + dot(hb[m], d[m])
                if sweep == ITERS - 1:
                    outs[m][...] = jnp.where(keep, kept[m][...], (new * final[m]).astype(bf16))
                    continue
                h[m] = new
                hb[m] = new.astype(bf16)
            square = dot(d[m], d[m]) if sweep > 0 else dot(wide[m], tall[m])
            w[m] = square
            q[m] = square.astype(bf16)
        if sweep == ITERS - 1:
            break
        for m in both:
            cube = dot(d[m], q[m])
            square = w[m]
            u[m] = (3.75 * square + cube).astype(bf16)
            w[m] = 2.5 * square + 5.0 * cube
        for m in both:
            d[m] = (w[m] + dot(q[m], u[m])).astype(bf16)


def step_kernel(owner_slot, refresh, partials_hbm, left_stat_hbm, right_stat_hbm, left_root_hbm, right_root_hbm,
                out, left_new, right_new, left_out, right_out,
                partials, left_stat, right_stat, left_root, right_root, g, update,
                st, ra1, ra2, ra3, rb1, sb, rb2, rb3, acc_a, acc_b, sum_a, send_sem, recv_sem, load_sem, *root_scratch):
    loads = [pltpu.make_async_copy(partials_hbm.at[i], partials.at[i], load_sem.at[i]) for i in range(SLOTS)]
    stats = [pltpu.make_async_copy(src, dst, load_sem.at[SLOTS + i]) for i, (src, dst) in enumerate((
        (left_stat_hbm, left_stat), (right_stat_hbm, right_stat), (left_root_hbm, left_root), (right_root_hbm, right_root)))]
    for copy in loads:
        copy.start()
    x, yl, yh, z, c = position()
    dp, ow = lax.axis_index("dp"), lax.axis_index("owner")

    def owner(dz, dy, dc=0):
        return (((yh + dy) % 2) * ZS + (z + dz) % ZS) * 2 + (c + dc) % 2

    xp = (((x + 1) % XS) * 2 + yl, ow)
    xm = (((x + XS - 1) % XS) * 2 + yl, ow)
    yo = (x * 2 + 1 - yl, ow)
    zp, zm = (dp, owner(1, 0)), (dp, owner(3, 0))
    yp, co = (dp, owner(0, 1)), (dp, owner(0, 0, 1))
    greet((xp, xm, yo, zp, zm, yp, co))
    for copy in loads:
        copy.wait()
    go = Copies(send_sem, recv_sem)

    def block_of(dx, dy):
        slot = ((x + dx) % XS) * 2 + (yl + dy) % 2
        found = jnp.int32(0)
        for r in range(SLOTS):
            found = jnp.where(owner_slot[r, ow] == slot, jnp.int32(r), found)
        return found

    where = {(dx, dy): block_of(dx, dy) for dx in range(XS) for dy in range(2)}

    def stage(dx, dy, rows):
        st[dx * 2 + dy, rows, :] = partials[where[dx, dy], rows, :]

    def own(dx, dy, rows):
        return st.at[dx * 2 + dy, rows]

    def first_a(dy):
        stage(2, dy, A_ALL)
        go.start(("a1p", dy), own(2, dy, A_LO), ra1.at[0, dy], xp)
        go.start(("a1m", dy), own(2, dy, A_HI), ra1.at[1, dy], xm)

    def own_a(dy):
        stage(1, dy, A_ALL)
        go.start(("a2p", dy), own(1, dy, A_HI), ra2.at[0, dy, HI_A], xp)
        stage(3, dy, A_ALL)
        go.start(("a2m", dy), own(3, dy, A_LO), ra2.at[1, dy, LO_A], xm)

    def sum_of_a(dy):
        go.arrived(("a1p", dy), ("a1m", dy))
        acc_a[0, dy] = (st[2 + dy, A_LO, :].astype(f32) + ra1[0, dy].astype(f32)).astype(bf16)
        go.start(("a3p", dy), acc_a.at[0, dy], ra2.at[0, dy, LO_A], xp)
        acc_a[1, dy] = (st[6 + dy, A_HI, :].astype(f32) + ra1[1, dy].astype(f32)).astype(bf16)
        go.start(("a3m", dy), acc_a.at[1, dy], ra2.at[1, dy, HI_A], xm)

    def first_b(dx):
        stage(dx, 1, B_ALL)
        go.start(("b1", dx), own(dx, 1, B_ALL), rb1.at[dx], yo)

    def sum_of_b(dx):
        stage(dx, 0, B_ALL)
        go.arrived(("b1", dx))
        sb[dx] = (st[dx * 2, B_ALL, :].astype(f32) + rb1[dx].astype(f32)).astype(bf16)

    first_a(1)
    for copy in stats:
        copy.start()
    first_b(2)
    first_a(0)
    own_a(1)
    first_b(1)
    stage(0, 0, A_ALL)
    stage(0, 1, A_ALL)
    sum_of_a(1)
    sum_of_b(2)
    first_b(3)
    own_a(0)
    sum_of_a(0)
    go.start("b2p", sb.at[2, LO_B], rb2.at[0], xp)
    go.start("b2m", sb.at[2, HI_B], rb2.at[1], xm)
    sum_of_b(1)
    first_b(0)
    go.start("b3p", sb.at[1, HI_B], rb3.at[0, HI_B], xp)
    go.arrived(("a2p", 1), ("a2m", 1), ("a3p", 1), ("a3m", 1))
    sum_a[...] = (st[1, A_ALL, :].astype(f32) + ra2[0, 1].astype(f32) + ra2[1, 1].astype(f32)).astype(bf16)
    go.start("a4", sum_a, ra3, yo)
    sum_of_b(3)
    go.start("b3m", sb.at[3, LO_B], rb3.at[1, LO_B], xm)
    go.arrived("b2p", "b2m")
    acc_b[0] = (sb[1, LO_B, :].astype(f32) + rb2[0].astype(f32)).astype(bf16)
    go.start("b4p", acc_b.at[0], rb3.at[0, LO_B], xp)
    acc_b[1] = (sb[3, HI_B, :].astype(f32) + rb2[1].astype(f32)).astype(bf16)
    go.start("b4m", acc_b.at[1], rb3.at[1, HI_B], xm)
    go.arrived(("a2p", 0), ("a2m", 0), ("a3p", 0), ("a3m", 0))
    stage(0, 0, B_ALL)
    go.arrived(("b1", 0))
    go.arrived("a4")
    g[A_ALL, :] = (st[0, A_ALL, :].astype(f32) + ra2[0, 0].astype(f32) + ra2[1, 0].astype(f32)
                       + ra3[...].astype(f32)).astype(bf16)
    go.arrived("b3p", "b3m", "b4p", "b4m")
    g[B_ALL, :] = (st[0, B_ALL, :].astype(f32) + rb1[0].astype(f32) + rb3[0].astype(f32)
                       + rb3[1].astype(f32)).astype(bf16)

    block = ow * SLOTS
    for r in range(SLOTS):
        block = jnp.where(owner_slot[r, ow] == dp, ow * SLOTS + r, block)
    hits = jnp.int32(0)
    for i in range(REFRESH):
        hits = hits + jnp.where(refresh[i] == block, jnp.int32(1), jnp.int32(0))
    for copy in stats:
        copy.wait()
    low = g[...]
    low_t = low.T
    weight = (1.0 - decay_rate) / N
    left_new[...] = decay_rate * left_stat[...] + weight * dot(low, low_t)
    right_new[...] = decay_rate * right_stat[...] + weight * dot(low_t, low)
    roots((left_new, right_new), hits == 0, (left_root, right_root), (left_out, right_out), *root_scratch)
    raw = dot(dot(left_out[...], low).astype(bf16), right_out[...])
    full = low.astype(f32)
    graft = jnp.sqrt(total(full * full) * (1.0 / (N * N))) / jnp.sqrt(total(raw * raw) * (1.0 / (N * N)) + graft_eps)
    update[...] = (raw * graft).astype(bf16)

    def pass_on(name, dz, dy, rows, target):
        piece = out.at[owner(dz, dy), rows]
        go.start(name, piece, piece, target)

    def share(dz, dy, rows, tag):
        pass_on(("core", dz, dy, tag), dz, dy, rows, co)

    def mine(name, rows, target):
        go.start(name, update.at[rows], out.at[owner(0, 0), rows], target)

    mine("yY", Y_ALL, yp)
    mine("zZ+", Z_ALL, zp)
    mine("zZ-", Z_ALL, zm)
    mine("zY+", Y_ALL, zp)
    mine("zY-", Y_ALL, zm)
    mine("yZ", Z_ALL, yp)
    mine("core", pl.ds(0, N), co)
    out[owner(0, 0)] = update[...]

    go.arrived("zZ+")
    pass_on("zZ2+", 3, 0, Z_LO, zp)
    pass_on("yZ-", 3, 0, Z_ALL, yp)
    share(3, 0, Z_ALL, "Z")
    go.arrived("zZ-")
    pass_on("zZ2-", 1, 0, Z_HI, zm)
    pass_on("yZ+", 1, 0, Z_ALL, yp)
    share(1, 0, Z_ALL, "Z")
    go.arrived("yY")
    pass_on("pY+", 0, 1, Y_ALL, zp)
    pass_on("pY-", 0, 1, Y_ALL, zm)
    share(0, 1, Y_ALL, "Y")
    go.arrived("zY+")
    pass_on("zY2+", 3, 0, Y_LO, zp)
    share(3, 0, Y_ALL, "Y")
    go.arrived("zY-")
    pass_on("zY2-", 1, 0, Y_HI, zm)
    share(1, 0, Y_ALL, "Y")
    go.arrived("yZ")
    share(0, 1, Z_ALL, "Z")
    go.arrived("zZ2+", "zZ2-")
    pass_on("yZ2", 2, 0, Z_ALL, yp)
    share(2, 0, Z_ALL, "Z")
    go.arrived("yZ-")
    share(3, 1, Z_ALL, "Z")
    go.arrived("pY+")
    pass_on("pY2+", 3, 1, Y_LO, zp)
    share(3, 1, Y_ALL, "Y")
    go.arrived("pY-")
    pass_on("pY2-", 1, 1, Y_HI, zm)
    share(1, 1, Y_ALL, "Y")
    go.arrived("yZ+")
    share(1, 1, Z_ALL, "Z")
    go.arrived("zY2+", "zY2-")
    share(2, 0, Y_ALL, "Y")
    go.arrived("yZ2")
    share(2, 1, Z_ALL, "Z")
    go.arrived("pY2+", "pY2-")
    share(2, 1, Y_ALL, "Y")
    go.arrived("core", *[name for name in go.started if name[0] == "core" and len(name) == 4 and name != "core"])
    go.finish()


def whole_step(*arrays):
    vmem, smem, hbm = (pl.BlockSpec(memory_space=space) for space in (pltpu.VMEM, pltpu.SMEM, pltpu.HBM))
    like = lambda dtype, *lead: pltpu.VMEM(lead + (N, N), dtype)
    vm = lambda *shape: pltpu.VMEM(shape + (N,), bf16)
    copies = 23 + 33
    return pl.pallas_call(
        step_kernel,
        out_shape=(like(bf16, 16), like(f32), like(f32), like(bf16), like(bf16)),
        in_specs=[smem] * 2 + [hbm] * 5,
        out_specs=[vmem] * 5,
        scratch_shapes=[
            vm(SLOTS, N), pltpu.VMEM((N, N), f32), pltpu.VMEM((N, N), f32), vm(N), vm(N), vm(N), vm(N),
            vm(SLOTS, N), vm(2, 2, RAH), vm(2, 2, RA), vm(RA), vm(XS, RB), vm(XS, RB), vm(2, RBH), vm(2, RB),
            vm(2, 2, RAH), vm(2, RBH), vm(RA),
            pltpu.SemaphoreType.DMA((copies,)), pltpu.SemaphoreType.DMA((copies,)), pltpu.SemaphoreType.DMA((SLOTS + 4,)),
            *[pltpu.VMEM((2, N, N), dtype) for dtype in (bf16, bf16, bf16, bf16, f32, f32)],
            pltpu.VMEM((2, N, 3 * N), bf16), pltpu.VMEM((2, 3 * N, N), bf16),
        ],
        compiler_params=pltpu.CompilerParams(collective_id=0, has_side_effects=True, vmem_limit_bytes=44 * 2**20),
        name="whole_step",
    )(*arrays)


def write_kernel(*refs):
    count = len(refs) // 2
    sems = refs[-1]
    copies, at = [], 0
    for src, dst in zip(refs[:count], refs[count:-1]):
        parts = [(src.at[i], dst.at[i]) for i in range(src.shape[0])] if len(src.shape) == 3 else [(src, dst)]
        for part in parts:
            copies.append(pltpu.make_async_copy(*part, sems.at[at]))
            copies[-1].start()
            at += 1
    for copy in copies:
        copy.wait()


def write_out(arrays):
    return pl.pallas_call(
        write_kernel,
        out_shape=tuple(jax.ShapeDtypeStruct(a.shape, a.dtype) for a in arrays),
        in_specs=[pl.BlockSpec(memory_space=pltpu.VMEM)] * len(arrays),
        out_specs=[pl.BlockSpec(memory_space=pl.ANY)] * len(arrays),
        scratch_shapes=[pltpu.SemaphoreType.DMA((20,))],
        compiler_params=pltpu.CompilerParams(vmem_limit_bytes=2**20),
        name="write_out",
    )(*arrays)


def body(grad_partials, owner_slot, refresh_blocks, left_stat, right_stat, left_root, right_root):
    results = whole_step(owner_slot.T, refresh_blocks, grad_partials[0], left_stat[0, 0], right_stat[0, 0], left_root[0, 0], right_root[0, 0])
    update, *own = write_out(results)
    return (update[:, None], *(array[None, None] for array in own))


def solution(mesh):
    slots = P("owner", "dp", None, None)
    return jax.shard_map(
        body,
        mesh=mesh,
        in_specs=(P("dp", "owner", None, None), P(), P(), slots, slots, slots, slots),
        out_specs=(P(None, "dp", None, None), slots, slots, slots, slots),
        check_vma=False,
    )
```

```python
import jax
import jax.numpy as jnp
from jax import lax
from jax.experimental import pallas as pl
from jax.experimental.pallas import tpu as pltpu
from jax.sharding import PartitionSpec as P

MESH = pl.DeviceIdType.MESH
f32 = jnp.float32
bf16 = jnp.bfloat16

N = 512
XS, ZS, SLOTS, REFRESH = 4, 4, 8, 32
ITERS = 4
decay_rate = 0.8
graft_eps = 1e-06

RA, RAH = 288, 144
RB, RBH = N - RA, (N - RA) // 2
A_LO, A_HI, A_ALL = pl.ds(0, RAH), pl.ds(RAH, RAH), pl.ds(0, RA)
B_LO, B_HI, B_ALL = pl.ds(RA, RBH), pl.ds(RA + RBH, RBH), pl.ds(RA, RB)
LO_A, HI_A = pl.ds(0, RAH), pl.ds(RAH, RAH)
LO_B, HI_B = pl.ds(0, RBH), pl.ds(RBH, RBH)


def position():
    dp, ow = lax.axis_index("dp"), lax.axis_index("owner")
    return dp // 2, dp % 2, ow // 8, (ow // 2) % 4, ow % 2


def greet(targets):
    barrier = pltpu.get_barrier_semaphore()
    for target in targets:
        pl.semaphore_signal(barrier, inc=1, device_id=target, device_id_type=MESH)
    pl.semaphore_wait(barrier, len(targets))


class Copies:
    def __init__(self, send_sem, recv_sem):
        self.send_sem, self.recv_sem, self.started = send_sem, recv_sem, {}

    def start(self, name, src, dst, target):
        at = len(self.started)
        copy = pltpu.make_async_remote_copy(
            src_ref=src, dst_ref=dst, send_sem=self.send_sem.at[at], recv_sem=self.recv_sem.at[at],
            device_id=target, device_id_type=MESH)
        copy.start()
        self.started[name] = copy

    def arrived(self, *names):
        for name in names:
            self.started[name].wait_recv()

    def finish(self):
        for copy in self.started.values():
            copy.wait_send()


RY, RYH = 288, 144
RZ, RZH = N - RY, (N - RY) // 2
Y_ALL, Y_LO, Y_HI = pl.ds(0, RY), pl.ds(0, RYH), pl.ds(RYH, RYH)
Z_ALL, Z_LO, Z_HI = pl.ds(RY, RZ), pl.ds(RY, RZH), pl.ds(RY + RZH, RZH)


def dot(a, b):
    return jnp.dot(a, b, preferred_element_type=f32)


def split(a):
    high = a.astype(bf16)
    return high, (a - high.astype(f32)).astype(bf16)


def total(a):
    return jnp.sum(jnp.sum(a, axis=0, keepdims=True), axis=1, keepdims=True)


def roots(stats, outs, d, q, u, hb, h, w, wide, tall):
    rows = lax.broadcasted_iota(jnp.int32, (N, N), 0)
    cols = lax.broadcasted_iota(jnp.int32, (N, N), 1)
    both = range(2)
    final = []
    for m in both:
        eye = jnp.where(rows == cols, 1.0, 0.0).astype(f32)
        stat = stats[m][...]
        scale = total(stat * eye) * (2.0 / N)
        final.append(lax.rsqrt(jnp.sqrt(scale)))
        first = (eye - stat * (1.0 / scale)) * 0.25
        high, rest = split(first)
        d[m] = high
        h[m] = eye + first
        hb[m] = (eye + first).astype(bf16)
        wide[m, :, 0:N], wide[m, :, N:2 * N], wide[m, :, 2 * N:3 * N] = high, high, rest
        tall[m, 0:N, :], tall[m, N:2 * N, :], tall[m, 2 * N:3 * N, :] = high, rest, high
    for sweep in range(ITERS):
        for m in both:
            if sweep > 0:
                new = h[m] + dot(hb[m], d[m])
                if sweep == ITERS - 1:
                    outs[m][...] = (new * final[m]).astype(bf16)
                    continue
                h[m] = new
                hb[m] = new.astype(bf16)
            square = dot(d[m], d[m]) if sweep > 0 else dot(wide[m], tall[m])
            w[m] = square
            q[m] = square.astype(bf16)
        if sweep == ITERS - 1:
            break
        for m in both:
            cube = dot(d[m], q[m])
            square = w[m]
            u[m] = (3.75 * square + cube).astype(bf16)
            w[m] = 2.5 * square + 5.0 * cube
        for m in both:
            d[m] = (w[m] + dot(q[m], u[m])).astype(bf16)


def reduce_kernel(owner_slot, partials_hbm, left_stat_hbm, right_stat_hbm, left_root_hbm, right_root_hbm,
                  g, left_stat, right_stat, left_root, right_root,
                  partials, st, ra1, ra2, ra3, rb1, sb, rb2, rb3, acc_a, acc_b, sum_a, send_sem, recv_sem, load_sem):
    loads = [pltpu.make_async_copy(partials_hbm.at[i], partials.at[i], load_sem.at[i]) for i in range(SLOTS)]
    stats = [pltpu.make_async_copy(src, dst, load_sem.at[SLOTS + i]) for i, (src, dst) in enumerate((
        (left_stat_hbm, left_stat), (right_stat_hbm, right_stat), (left_root_hbm, left_root), (right_root_hbm, right_root)))]
    for copy in loads:
        copy.start()
    x, yl, yh, z, c = position()
    dp, ow = lax.axis_index("dp"), lax.axis_index("owner")
    xp = (((x + 1) % XS) * 2 + yl, ow)
    xm = (((x + XS - 1) % XS) * 2 + yl, ow)
    yo = (x * 2 + 1 - yl, ow)
    greet((xp, xm, yo))
    for copy in loads:
        copy.wait()
    go = Copies(send_sem, recv_sem)

    def block_of(dx, dy):
        slot = ((x + dx) % XS) * 2 + (yl + dy) % 2
        found = jnp.int32(0)
        for r in range(SLOTS):
            found = jnp.where(owner_slot[r, ow] == slot, jnp.int32(r), found)
        return found

    where = {(dx, dy): block_of(dx, dy) for dx in range(XS) for dy in range(2)}

    def stage(dx, dy, rows):
        st[dx * 2 + dy, rows, :] = partials[where[dx, dy], rows, :]

    def part(dx, dy, rows):
        return st.at[dx * 2 + dy, rows]

    def first_a(dy):
        stage(2, dy, A_ALL)
        go.start(("a1p", dy), part(2, dy, A_LO), ra1.at[0, dy], xp)
        go.start(("a1m", dy), part(2, dy, A_HI), ra1.at[1, dy], xm)

    def own_a(dy):
        stage(1, dy, A_ALL)
        go.start(("a2p", dy), part(1, dy, A_HI), ra2.at[0, dy, HI_A], xp)
        stage(3, dy, A_ALL)
        go.start(("a2m", dy), part(3, dy, A_LO), ra2.at[1, dy, LO_A], xm)

    def sum_of_a(dy):
        go.arrived(("a1p", dy), ("a1m", dy))
        acc_a[0, dy] = (st[2 + dy, A_LO, :].astype(f32) + ra1[0, dy].astype(f32)).astype(bf16)
        go.start(("a3p", dy), acc_a.at[0, dy], ra2.at[0, dy, LO_A], xp)
        acc_a[1, dy] = (st[6 + dy, A_HI, :].astype(f32) + ra1[1, dy].astype(f32)).astype(bf16)
        go.start(("a3m", dy), acc_a.at[1, dy], ra2.at[1, dy, HI_A], xm)

    def first_b(dx):
        stage(dx, 1, B_ALL)
        go.start(("b1", dx), part(dx, 1, B_ALL), rb1.at[dx], yo)

    def sum_of_b(dx):
        stage(dx, 0, B_ALL)
        go.arrived(("b1", dx))
        sb[dx] = (st[dx * 2, B_ALL, :].astype(f32) + rb1[dx].astype(f32)).astype(bf16)

    first_a(1)
    for copy in stats:
        copy.start()
    first_b(2)
    first_a(0)
    own_a(1)
    first_b(1)
    stage(0, 0, A_ALL)
    stage(0, 1, A_ALL)
    sum_of_a(1)
    sum_of_b(2)
    first_b(3)
    own_a(0)
    sum_of_a(0)
    go.start("b2p", sb.at[2, LO_B], rb2.at[0], xp)
    go.start("b2m", sb.at[2, HI_B], rb2.at[1], xm)
    sum_of_b(1)
    first_b(0)
    go.start("b3p", sb.at[1, HI_B], rb3.at[0, HI_B], xp)
    go.arrived(("a2p", 1), ("a2m", 1), ("a3p", 1), ("a3m", 1))
    sum_a[...] = (st[1, A_ALL, :].astype(f32) + ra2[0, 1].astype(f32) + ra2[1, 1].astype(f32)).astype(bf16)
    go.start("a4", sum_a, ra3, yo)
    sum_of_b(3)
    go.start("b3m", sb.at[3, LO_B], rb3.at[1, LO_B], xm)
    go.arrived("b2p", "b2m")
    acc_b[0] = (sb[1, LO_B, :].astype(f32) + rb2[0].astype(f32)).astype(bf16)
    go.start("b4p", acc_b.at[0], rb3.at[0, LO_B], xp)
    acc_b[1] = (sb[3, HI_B, :].astype(f32) + rb2[1].astype(f32)).astype(bf16)
    go.start("b4m", acc_b.at[1], rb3.at[1, HI_B], xm)
    go.arrived(("a2p", 0), ("a2m", 0), ("a3p", 0), ("a3m", 0))
    stage(0, 0, B_ALL)
    go.arrived(("b1", 0))
    go.arrived("a4")
    g[A_ALL, :] = (st[0, A_ALL, :].astype(f32) + ra2[0, 0].astype(f32) + ra2[1, 0].astype(f32)
                       + ra3[...].astype(f32)).astype(bf16)
    go.arrived("b3p", "b3m", "b4p", "b4m")
    g[B_ALL, :] = (st[0, B_ALL, :].astype(f32) + rb1[0].astype(f32) + rb3[0].astype(f32)
                       + rb3[1].astype(f32)).astype(bf16)
    for copy in stats:
        copy.wait()
    go.finish()


vmem, smem, hbm = (pl.BlockSpec(memory_space=space) for space in (pltpu.VMEM, pltpu.SMEM, pltpu.HBM))


def own(space, dtype, *lead):
    return space(lead + (N, N), dtype)


def reduce_scatter(*arrays):
    vm = lambda *shape: pltpu.VMEM(shape + (N,), bf16)
    return pl.pallas_call(
        reduce_kernel,
        out_shape=tuple(own(pltpu.VMEM, dtype) for dtype in (bf16, f32, f32, bf16, bf16)),
        in_specs=[smem] + [hbm] * 5,
        out_specs=[vmem] * 5,
        scratch_shapes=[
            vm(SLOTS, N), vm(SLOTS, N), vm(2, 2, RAH), vm(2, 2, RA), vm(RA), vm(XS, RB), vm(XS, RB), vm(2, RBH), vm(2, RB),
            vm(2, 2, RAH), vm(2, RBH), vm(RA),
            pltpu.SemaphoreType.DMA((23,)), pltpu.SemaphoreType.DMA((23,)), pltpu.SemaphoreType.DMA((SLOTS + 4,)),
        ],
        compiler_params=pltpu.CompilerParams(collective_id=0, has_side_effects=True, vmem_limit_bytes=24 * 2**20),
        name="reduce_scatter",
    )(*arrays)


def local_kernel(owner_slot, refresh, g, left_stat, right_stat, left_root, right_root,
                 update, left_new_hbm, right_new_hbm, left_out_hbm, right_out_hbm,
                 left_new, right_new, left_out, right_out, sems, *root_scratch):
    dp, ow = lax.axis_index("dp"), lax.axis_index("owner")
    writes = [pltpu.make_async_copy(src, dst, sems.at[i]) for i, (src, dst) in enumerate((
        (left_new, left_new_hbm), (right_new, right_new_hbm), (left_out, left_out_hbm), (right_out, right_out_hbm)))]
    block = ow * SLOTS
    for r in range(SLOTS):
        block = jnp.where(owner_slot[r, ow] == dp, ow * SLOTS + r, block)
    hits = jnp.int32(0)
    for i in range(REFRESH):
        hits = hits + jnp.where(refresh[i] == block, jnp.int32(1), jnp.int32(0))
    low = g[...]
    low_t = low.T
    weight = (1.0 - decay_rate) / N
    left_new[...] = decay_rate * left_stat[...] + weight * dot(low, low_t)
    right_new[...] = decay_rate * right_stat[...] + weight * dot(low_t, low)
    writes[0].start()
    writes[1].start()

    @pl.when(hits > 0)
    def _():
        roots((left_new, right_new), (left_out, right_out), *root_scratch)

    @pl.when(hits == 0)
    def _():
        left_out[...] = left_root[...]
        right_out[...] = right_root[...]

    writes[2].start()
    writes[3].start()
    raw = dot(dot(left_out[...], low).astype(bf16), right_out[...])
    full = low.astype(f32)
    graft = jnp.sqrt(total(full * full) * (1.0 / (N * N))) / jnp.sqrt(total(raw * raw) * (1.0 / (N * N)) + graft_eps)
    update[...] = (raw * graft).astype(bf16)
    for copy in writes:
        copy.wait()


def local_step(*arrays):
    mine = (bf16, f32, f32, bf16, bf16)
    return pl.pallas_call(
        local_kernel,
        out_shape=(own(pltpu.VMEM, bf16),) + tuple(own(pltpu.HBM, dtype) for dtype in mine[1:]),
        in_specs=[smem] * 2 + [vmem] * 5,
        out_specs=[vmem] + [hbm] * 4,
        scratch_shapes=[own(pltpu.VMEM, dtype) for dtype in mine[1:]] + [pltpu.SemaphoreType.DMA((4,))]
        + [own(pltpu.VMEM, dtype, 2) for dtype in (bf16, bf16, bf16, bf16, f32, f32)]
        + [pltpu.VMEM((2, N, 3 * N), bf16), pltpu.VMEM((2, 3 * N, N), bf16)],
        compiler_params=pltpu.CompilerParams(vmem_limit_bytes=32 * 2**20),
        name="local_step",
    )(*arrays)


def gather_kernel(update, out, send_sem, recv_sem):
    x, yl, yh, z, c = position()
    dp, ow = lax.axis_index("dp"), lax.axis_index("owner")

    def owner(dz, dy, dc=0):
        return (((yh + dy) % 2) * ZS + (z + dz) % ZS) * 2 + (c + dc) % 2

    zp, zm = (dp, owner(1, 0)), (dp, owner(3, 0))
    yp, co = (dp, owner(0, 1)), (dp, owner(0, 0, 1))
    greet((zp, zm, yp, co))
    go = Copies(send_sem, recv_sem)

    def pass_on(name, dz, dy, rows, target):
        piece = out.at[owner(dz, dy), rows]
        go.start(name, piece, piece, target)

    def share(dz, dy, rows, tag):
        pass_on(("core", dz, dy, tag), dz, dy, rows, co)

    def mine(name, rows, target):
        go.start(name, update.at[rows], out.at[owner(0, 0), rows], target)

    mine("yY", Y_ALL, yp)
    mine("zZ+", Z_ALL, zp)
    mine("zZ-", Z_ALL, zm)
    mine("zY+", Y_ALL, zp)
    mine("zY-", Y_ALL, zm)
    mine("yZ", Z_ALL, yp)
    mine("core", pl.ds(0, N), co)
    out[owner(0, 0)] = update[...]

    go.arrived("zZ+")
    pass_on("zZ2+", 3, 0, Z_LO, zp)
    pass_on("yZ-", 3, 0, Z_ALL, yp)
    share(3, 0, Z_ALL, "Z")
    go.arrived("zZ-")
    pass_on("zZ2-", 1, 0, Z_HI, zm)
    pass_on("yZ+", 1, 0, Z_ALL, yp)
    share(1, 0, Z_ALL, "Z")
    go.arrived("yY")
    pass_on("pY+", 0, 1, Y_ALL, zp)
    pass_on("pY-", 0, 1, Y_ALL, zm)
    share(0, 1, Y_ALL, "Y")
    go.arrived("zY+")
    pass_on("zY2+", 3, 0, Y_LO, zp)
    share(3, 0, Y_ALL, "Y")
    go.arrived("zY-")
    pass_on("zY2-", 1, 0, Y_HI, zm)
    share(1, 0, Y_ALL, "Y")
    go.arrived("yZ")
    share(0, 1, Z_ALL, "Z")
    go.arrived("zZ2+", "zZ2-")
    pass_on("yZ2", 2, 0, Z_ALL, yp)
    share(2, 0, Z_ALL, "Z")
    go.arrived("yZ-")
    share(3, 1, Z_ALL, "Z")
    go.arrived("pY+")
    pass_on("pY2+", 3, 1, Y_LO, zp)
    share(3, 1, Y_ALL, "Y")
    go.arrived("pY-")
    pass_on("pY2-", 1, 1, Y_HI, zm)
    share(1, 1, Y_ALL, "Y")
    go.arrived("yZ+")
    share(1, 1, Z_ALL, "Z")
    go.arrived("zY2+", "zY2-")
    share(2, 0, Y_ALL, "Y")
    go.arrived("yZ2")
    share(2, 1, Z_ALL, "Z")
    go.arrived("pY2+", "pY2-")
    share(2, 1, Y_ALL, "Y")
    go.arrived("core", *[name for name in go.started if name[0] == "core" and len(name) == 4 and name != "core"])
    go.finish()


def all_gather(update):
    return pl.pallas_call(
        gather_kernel,
        out_shape=own(pltpu.VMEM, bf16, 16),
        in_specs=[vmem],
        out_specs=vmem,
        scratch_shapes=[pltpu.SemaphoreType.DMA((33,)), pltpu.SemaphoreType.DMA((33,))],
        compiler_params=pltpu.CompilerParams(collective_id=1, has_side_effects=True, vmem_limit_bytes=2 * 2**20),
        name="all_gather",
    )(update)


def write_kernel(src, dst, sems):
    copies = [pltpu.make_async_copy(src.at[i], dst.at[i], sems.at[i]) for i in range(16)]
    for copy in copies:
        copy.start()
    for copy in copies:
        copy.wait()


def write_out(gathered):
    return pl.pallas_call(
        write_kernel,
        out_shape=own(pltpu.HBM, bf16, 16),
        in_specs=[vmem],
        out_specs=hbm,
        scratch_shapes=[pltpu.SemaphoreType.DMA((16,))],
        compiler_params=pltpu.CompilerParams(vmem_limit_bytes=2**20),
        name="write_out",
    )(gathered)


def body(grad_partials, owner_slot, refresh_blocks, left_stat, right_stat, left_root, right_root):
    table = owner_slot.T
    reduced = reduce_scatter(table, grad_partials[0], left_stat[0, 0], right_stat[0, 0], left_root[0, 0], right_root[0, 0])
    update, *mine = local_step(table, refresh_blocks, *reduced)
    gathered = write_out(all_gather(update))
    return (gathered[:, None], *(array[None, None] for array in mine))


def solution(mesh):
    slots = P("owner", "dp", None, None)
    return jax.shard_map(
        body,
        mesh=mesh,
        in_specs=(P("dp", "owner", None, None), P(), P(), slots, slots, slots, slots),
        out_specs=(P(None, "dp", None, None), slots, slots, slots, slots),
        check_vma=False,
    )
```

```python
import jax
import jax.numpy as jnp
from jax import lax
from jax.experimental import pallas as pl
from jax.experimental.pallas import tpu as pltpu
from jax.sharding import PartitionSpec as P

MESH = pl.DeviceIdType.MESH
f32 = jnp.float32
bf16 = jnp.bfloat16

N = 512
XS, ZS, SLOTS, REFRESH = 4, 4, 8, 32
ITERS = 4
decay_rate = 0.8
graft_eps = 1e-06

RA, RAH = 288, 144
RB, RBH = N - RA, (N - RA) // 2
A_LO, A_HI, A_ALL = pl.ds(0, RAH), pl.ds(RAH, RAH), pl.ds(0, RA)
B_LO, B_HI, B_ALL = pl.ds(RA, RBH), pl.ds(RA + RBH, RBH), pl.ds(RA, RB)
LO_A, HI_A = pl.ds(0, RAH), pl.ds(RAH, RAH)
LO_B, HI_B = pl.ds(0, RBH), pl.ds(RBH, RBH)


def position():
    dp, ow = lax.axis_index("dp"), lax.axis_index("owner")
    return dp // 2, dp % 2, ow // 8, (ow // 2) % 4, ow % 2


def greet(targets):
    barrier = pltpu.get_barrier_semaphore()
    for target in targets:
        pl.semaphore_signal(barrier, inc=1, device_id=target, device_id_type=MESH)
    pl.semaphore_wait(barrier, len(targets))


class Copies:
    def __init__(self, send_sem, recv_sem):
        self.send_sem, self.recv_sem, self.started = send_sem, recv_sem, {}

    def start(self, name, src, dst, target):
        at = len(self.started)
        copy = pltpu.make_async_remote_copy(
            src_ref=src, dst_ref=dst, send_sem=self.send_sem.at[at], recv_sem=self.recv_sem.at[at],
            device_id=target, device_id_type=MESH)
        copy.start()
        self.started[name] = copy

    def arrived(self, *names):
        for name in names:
            self.started[name].wait_recv()

    def finish(self):
        for copy in self.started.values():
            copy.wait_send()


RY, RYH = 288, 144
RZ, RZH = N - RY, (N - RY) // 2
Y_ALL, Y_LO, Y_HI = pl.ds(0, RY), pl.ds(0, RYH), pl.ds(RYH, RYH)
Z_ALL, Z_LO, Z_HI = pl.ds(RY, RZ), pl.ds(RY, RZH), pl.ds(RY + RZH, RZH)


def dot(a, b):
    return jnp.dot(a, b, preferred_element_type=f32)


def split(a):
    high = a.astype(bf16)
    return high, (a - high.astype(f32)).astype(bf16)


def total(a):
    return jnp.sum(jnp.sum(a, axis=0, keepdims=True), axis=1, keepdims=True)


def roots(stats, outs, d, q, u, hb, h, w, wide, tall):
    rows = lax.broadcasted_iota(jnp.int32, (N, N), 0)
    cols = lax.broadcasted_iota(jnp.int32, (N, N), 1)
    both = range(2)
    final = []
    for m in both:
        eye = jnp.where(rows == cols, 1.0, 0.0).astype(f32)
        stat = stats[m][...]
        scale = total(stat * eye) * (2.0 / N)
        final.append(lax.rsqrt(jnp.sqrt(scale)))
        first = (eye - stat * (1.0 / scale)) * 0.25
        high, rest = split(first)
        d[m] = high
        h[m] = eye + first
        hb[m] = (eye + first).astype(bf16)
        wide[m, :, 0:N], wide[m, :, N:2 * N], wide[m, :, 2 * N:3 * N] = high, high, rest
        tall[m, 0:N, :], tall[m, N:2 * N, :], tall[m, 2 * N:3 * N, :] = high, rest, high
    for sweep in range(ITERS):
        for m in both:
            if sweep > 0:
                new = h[m] + dot(hb[m], d[m])
                if sweep == ITERS - 1:
                    outs[m][...] = (new * final[m]).astype(bf16)
                    continue
                h[m] = new
                hb[m] = new.astype(bf16)
            square = dot(d[m], d[m]) if sweep > 0 else dot(wide[m], tall[m])
            w[m] = square
            q[m] = square.astype(bf16)
        if sweep == ITERS - 1:
            break
        for m in both:
            cube = dot(d[m], q[m])
            square = w[m]
            u[m] = (3.75 * square + cube).astype(bf16)
            w[m] = 2.5 * square + 5.0 * cube
        for m in both:
            d[m] = (w[m] + dot(q[m], u[m])).astype(bf16)


def reduce_kernel(owner_slot, refresh, partials_hbm, left_stat_hbm, right_stat_hbm, left_root_hbm, right_root_hbm,
                  hit, g, left_stat, right_stat, left_root, right_root,
                  partials, st, ra1, ra2, ra3, rb1, sb, rb2, rb3, acc_a, acc_b, sum_a, send_sem, recv_sem, load_sem):
    loads = [pltpu.make_async_copy(partials_hbm.at[i], partials.at[i], load_sem.at[i]) for i in range(SLOTS)]
    stats = [pltpu.make_async_copy(src, dst, load_sem.at[SLOTS + i]) for i, (src, dst) in enumerate((
        (left_stat_hbm, left_stat), (right_stat_hbm, right_stat), (left_root_hbm, left_root), (right_root_hbm, right_root)))]
    for copy in loads:
        copy.start()
    x, yl, yh, z, c = position()
    dp, ow = lax.axis_index("dp"), lax.axis_index("owner")
    xp = (((x + 1) % XS) * 2 + yl, ow)
    xm = (((x + XS - 1) % XS) * 2 + yl, ow)
    yo = (x * 2 + 1 - yl, ow)
    greet((xp, xm, yo))
    for copy in loads:
        copy.wait()
    go = Copies(send_sem, recv_sem)

    def block_of(dx, dy):
        slot = ((x + dx) % XS) * 2 + (yl + dy) % 2
        found = jnp.int32(0)
        for r in range(SLOTS):
            found = jnp.where(owner_slot[r, ow] == slot, jnp.int32(r), found)
        return found

    where = {(dx, dy): block_of(dx, dy) for dx in range(XS) for dy in range(2)}

    def stage(dx, dy, rows):
        st[dx * 2 + dy, rows, :] = partials[where[dx, dy], rows, :]

    def part(dx, dy, rows):
        return st.at[dx * 2 + dy, rows]

    def first_a(dy):
        stage(2, dy, A_ALL)
        go.start(("a1p", dy), part(2, dy, A_LO), ra1.at[0, dy], xp)
        go.start(("a1m", dy), part(2, dy, A_HI), ra1.at[1, dy], xm)

    def own_a(dy):
        stage(1, dy, A_ALL)
        go.start(("a2p", dy), part(1, dy, A_HI), ra2.at[0, dy, HI_A], xp)
        stage(3, dy, A_ALL)
        go.start(("a2m", dy), part(3, dy, A_LO), ra2.at[1, dy, LO_A], xm)

    def sum_of_a(dy):
        go.arrived(("a1p", dy), ("a1m", dy))
        acc_a[0, dy] = (st[2 + dy, A_LO, :].astype(f32) + ra1[0, dy].astype(f32)).astype(bf16)
        go.start(("a3p", dy), acc_a.at[0, dy], ra2.at[0, dy, LO_A], xp)
        acc_a[1, dy] = (st[6 + dy, A_HI, :].astype(f32) + ra1[1, dy].astype(f32)).astype(bf16)
        go.start(("a3m", dy), acc_a.at[1, dy], ra2.at[1, dy, HI_A], xm)

    def first_b(dx):
        stage(dx, 1, B_ALL)
        go.start(("b1", dx), part(dx, 1, B_ALL), rb1.at[dx], yo)

    def sum_of_b(dx):
        stage(dx, 0, B_ALL)
        go.arrived(("b1", dx))
        sb[dx] = (st[dx * 2, B_ALL, :].astype(f32) + rb1[dx].astype(f32)).astype(bf16)

    first_a(1)
    for copy in stats:
        copy.start()
    first_b(2)
    first_a(0)
    own_a(1)
    first_b(1)
    stage(0, 0, A_ALL)
    stage(0, 1, A_ALL)
    sum_of_a(1)
    sum_of_b(2)
    first_b(3)
    own_a(0)
    sum_of_a(0)
    go.start("b2p", sb.at[2, LO_B], rb2.at[0], xp)
    go.start("b2m", sb.at[2, HI_B], rb2.at[1], xm)
    sum_of_b(1)
    first_b(0)
    go.start("b3p", sb.at[1, HI_B], rb3.at[0, HI_B], xp)
    go.arrived(("a2p", 1), ("a2m", 1), ("a3p", 1), ("a3m", 1))
    sum_a[...] = (st[1, A_ALL, :].astype(f32) + ra2[0, 1].astype(f32) + ra2[1, 1].astype(f32)).astype(bf16)
    go.start("a4", sum_a, ra3, yo)
    sum_of_b(3)
    go.start("b3m", sb.at[3, LO_B], rb3.at[1, LO_B], xm)
    go.arrived("b2p", "b2m")
    acc_b[0] = (sb[1, LO_B, :].astype(f32) + rb2[0].astype(f32)).astype(bf16)
    go.start("b4p", acc_b.at[0], rb3.at[0, LO_B], xp)
    acc_b[1] = (sb[3, HI_B, :].astype(f32) + rb2[1].astype(f32)).astype(bf16)
    go.start("b4m", acc_b.at[1], rb3.at[1, HI_B], xm)
    go.arrived(("a2p", 0), ("a2m", 0), ("a3p", 0), ("a3m", 0))
    stage(0, 0, B_ALL)
    go.arrived(("b1", 0))
    go.arrived("a4")
    g[A_ALL, :] = (st[0, A_ALL, :].astype(f32) + ra2[0, 0].astype(f32) + ra2[1, 0].astype(f32)
                       + ra3[...].astype(f32)).astype(bf16)
    go.arrived("b3p", "b3m", "b4p", "b4m")
    g[B_ALL, :] = (st[0, B_ALL, :].astype(f32) + rb1[0].astype(f32) + rb3[0].astype(f32)
                       + rb3[1].astype(f32)).astype(bf16)
    block = ow * SLOTS
    for r in range(SLOTS):
        block = jnp.where(owner_slot[r, ow] == dp, ow * SLOTS + r, block)
    hits = jnp.int32(0)
    for i in range(REFRESH):
        hits = hits + jnp.where(refresh[i] == block, jnp.int32(1), jnp.int32(0))
    hit[0] = hits
    for copy in stats:
        copy.wait()
    go.finish()


vmem, smem, hbm = (pl.BlockSpec(memory_space=space) for space in (pltpu.VMEM, pltpu.SMEM, pltpu.HBM))


def own(space, dtype, *lead):
    return space(lead + (N, N), dtype)


def reduce_scatter(*arrays):
    vm = lambda *shape: pltpu.VMEM(shape + (N,), bf16)
    return pl.pallas_call(
        reduce_kernel,
        out_shape=(pltpu.SMEM((1,), jnp.int32),) + tuple(own(pltpu.VMEM, dtype) for dtype in (bf16, f32, f32, bf16, bf16)),
        in_specs=[smem] * 2 + [hbm] * 5,
        out_specs=[smem] + [vmem] * 5,
        scratch_shapes=[
            vm(SLOTS, N), vm(SLOTS, N), vm(2, 2, RAH), vm(2, 2, RA), vm(RA), vm(XS, RB), vm(XS, RB), vm(2, RBH), vm(2, RB),
            vm(2, 2, RAH), vm(2, RBH), vm(RA),
            pltpu.SemaphoreType.DMA((23,)), pltpu.SemaphoreType.DMA((23,)), pltpu.SemaphoreType.DMA((SLOTS + 4,)),
        ],
        compiler_params=pltpu.CompilerParams(collective_id=0, has_side_effects=True, vmem_limit_bytes=56 * 2**20),
        name="reduce_scatter",
    )(*arrays)


def local_kernel(hit, g, left_stat, right_stat, left_root, right_root,
                 update, left_new_hbm, right_new_hbm, left_out_hbm, right_out_hbm,
                 left_new, right_new, left_out, right_out, sems, *root_scratch):
    writes = [pltpu.make_async_copy(src, dst, sems.at[i]) for i, (src, dst) in enumerate((
        (left_new, left_new_hbm), (right_new, right_new_hbm), (left_out, left_out_hbm), (right_out, right_out_hbm)))]
    low = g[...]
    low_t = low.T
    weight = (1.0 - decay_rate) / N
    left_new[...] = decay_rate * left_stat[...] + weight * dot(low, low_t)
    right_new[...] = decay_rate * right_stat[...] + weight * dot(low_t, low)
    writes[0].start()
    writes[1].start()

    @pl.when(hit[0] > 0)
    def _():
        roots((left_new, right_new), (left_out, right_out), *root_scratch)

    @pl.when(hit[0] == 0)
    def _():
        left_out[...] = left_root[...]
        right_out[...] = right_root[...]

    writes[2].start()
    writes[3].start()
    raw = dot(dot(left_out[...], low).astype(bf16), right_out[...])
    full = low.astype(f32)
    graft = jnp.sqrt(total(full * full) * (1.0 / (N * N))) / jnp.sqrt(total(raw * raw) * (1.0 / (N * N)) + graft_eps)
    update[...] = (raw * graft).astype(bf16)
    for copy in writes:
        copy.wait()


def local_step(*arrays):
    mine = (bf16, f32, f32, bf16, bf16)
    return pl.pallas_call(
        local_kernel,
        out_shape=(own(pltpu.VMEM, bf16),) + tuple(own(pltpu.HBM, dtype) for dtype in mine[1:]),
        in_specs=[smem] + [vmem] * 5,
        out_specs=[vmem] + [hbm] * 4,
        scratch_shapes=[own(pltpu.VMEM, dtype) for dtype in mine[1:]] + [pltpu.SemaphoreType.DMA((4,))]
        + [own(pltpu.VMEM, dtype, 2) for dtype in (bf16, bf16, bf16, bf16, f32, f32)]
        + [pltpu.VMEM((2, N, 3 * N), bf16), pltpu.VMEM((2, 3 * N, N), bf16)],
        compiler_params=pltpu.CompilerParams(vmem_limit_bytes=48 * 2**20),
        name="local_step",
    )(*arrays)


def gather_kernel(update, out, send_sem, recv_sem):
    x, yl, yh, z, c = position()
    dp, ow = lax.axis_index("dp"), lax.axis_index("owner")

    def owner(dz, dy, dc=0):
        return (((yh + dy) % 2) * ZS + (z + dz) % ZS) * 2 + (c + dc) % 2

    zp, zm = (dp, owner(1, 0)), (dp, owner(3, 0))
    yp, co = (dp, owner(0, 1)), (dp, owner(0, 0, 1))
    greet((zp, zm, yp, co))
    go = Copies(send_sem, recv_sem)

    def pass_on(name, dz, dy, rows, target):
        piece = out.at[owner(dz, dy), rows]
        go.start(name, piece, piece, target)

    def share(dz, dy, rows, tag):
        pass_on(("core", dz, dy, tag), dz, dy, rows, co)

    def mine(name, rows, target):
        go.start(name, update.at[rows], out.at[owner(0, 0), rows], target)

    mine("yY", Y_ALL, yp)
    mine("zZ+", Z_ALL, zp)
    mine("zZ-", Z_ALL, zm)
    mine("zY+", Y_ALL, zp)
    mine("zY-", Y_ALL, zm)
    mine("yZ", Z_ALL, yp)
    mine("core", pl.ds(0, N), co)
    out[owner(0, 0)] = update[...]

    go.arrived("zZ+")
    pass_on("zZ2+", 3, 0, Z_LO, zp)
    pass_on("yZ-", 3, 0, Z_ALL, yp)
    share(3, 0, Z_ALL, "Z")
    go.arrived("zZ-")
    pass_on("zZ2-", 1, 0, Z_HI, zm)
    pass_on("yZ+", 1, 0, Z_ALL, yp)
    share(1, 0, Z_ALL, "Z")
    go.arrived("yY")
    pass_on("pY+", 0, 1, Y_ALL, zp)
    pass_on("pY-", 0, 1, Y_ALL, zm)
    share(0, 1, Y_ALL, "Y")
    go.arrived("zY+")
    pass_on("zY2+", 3, 0, Y_LO, zp)
    share(3, 0, Y_ALL, "Y")
    go.arrived("zY-")
    pass_on("zY2-", 1, 0, Y_HI, zm)
    share(1, 0, Y_ALL, "Y")
    go.arrived("yZ")
    share(0, 1, Z_ALL, "Z")
    go.arrived("zZ2+", "zZ2-")
    pass_on("yZ2", 2, 0, Z_ALL, yp)
    share(2, 0, Z_ALL, "Z")
    go.arrived("yZ-")
    share(3, 1, Z_ALL, "Z")
    go.arrived("pY+")
    pass_on("pY2+", 3, 1, Y_LO, zp)
    share(3, 1, Y_ALL, "Y")
    go.arrived("pY-")
    pass_on("pY2-", 1, 1, Y_HI, zm)
    share(1, 1, Y_ALL, "Y")
    go.arrived("yZ+")
    share(1, 1, Z_ALL, "Z")
    go.arrived("zY2+", "zY2-")
    share(2, 0, Y_ALL, "Y")
    go.arrived("yZ2")
    share(2, 1, Z_ALL, "Z")
    go.arrived("pY2+", "pY2-")
    share(2, 1, Y_ALL, "Y")
    go.arrived("core", *[name for name in go.started if name[0] == "core" and len(name) == 4 and name != "core"])
    go.finish()


def all_gather(update):
    return pl.pallas_call(
        gather_kernel,
        out_shape=own(pltpu.VMEM, bf16, 16),
        in_specs=[vmem],
        out_specs=vmem,
        scratch_shapes=[pltpu.SemaphoreType.DMA((33,)), pltpu.SemaphoreType.DMA((33,))],
        compiler_params=pltpu.CompilerParams(collective_id=1, has_side_effects=True, vmem_limit_bytes=2 * 2**20),
        name="all_gather",
    )(update)


def write_kernel(src, dst, sems):
    copies = [pltpu.make_async_copy(src.at[i], dst.at[i], sems.at[i]) for i in range(16)]
    for copy in copies:
        copy.start()
    for copy in copies:
        copy.wait()


def write_out(gathered):
    return pl.pallas_call(
        write_kernel,
        out_shape=own(pltpu.HBM, bf16, 16),
        in_specs=[vmem],
        out_specs=hbm,
        scratch_shapes=[pltpu.SemaphoreType.DMA((16,))],
        compiler_params=pltpu.CompilerParams(vmem_limit_bytes=2**20),
        name="write_out",
    )(gathered)


def body(grad_partials, owner_slot, refresh_blocks, left_stat, right_stat, left_root, right_root):
    reduced = reduce_scatter(owner_slot.T, refresh_blocks, grad_partials[0], left_stat[0, 0], right_stat[0, 0], left_root[0, 0], right_root[0, 0])
    update, *mine = local_step(*reduced)
    gathered = write_out(all_gather(update))
    return (gathered[:, None], *(array[None, None] for array in mine))


def solution(mesh):
    slots = P("owner", "dp", None, None)
    return jax.shard_map(
        body,
        mesh=mesh,
        in_specs=(P("dp", "owner", None, None), P(), P(), slots, slots, slots, slots),
        out_specs=(P(None, "dp", None, None), slots, slots, slots, slots),
        check_vma=False,
    )
```

```python
import jax
import jax.numpy as jnp
from jax import lax
from jax.experimental import pallas as pl
from jax.experimental.pallas import tpu as pltpu
from jax.sharding import PartitionSpec as P

MESH = pl.DeviceIdType.MESH
f32 = jnp.float32
bf16 = jnp.bfloat16

N = 512
XS, ZS, SLOTS, REFRESH = 4, 4, 8, 32
ITERS = 4
decay_rate = 0.8
graft_eps = 1e-06

RA, RAH = 288, 144
RB, RBH = N - RA, (N - RA) // 2
A_LO, A_HI, A_ALL = pl.ds(0, RAH), pl.ds(RAH, RAH), pl.ds(0, RA)
B_LO, B_HI, B_ALL = pl.ds(RA, RBH), pl.ds(RA + RBH, RBH), pl.ds(RA, RB)
LO_A, HI_A = pl.ds(0, RAH), pl.ds(RAH, RAH)
LO_B, HI_B = pl.ds(0, RBH), pl.ds(RBH, RBH)


def position():
    dp, ow = lax.axis_index("dp"), lax.axis_index("owner")
    return dp // 2, dp % 2, ow // 8, (ow // 2) % 4, ow % 2


def greet(targets):
    barrier = pltpu.get_barrier_semaphore()
    for target in targets:
        pl.semaphore_signal(barrier, inc=1, device_id=target, device_id_type=MESH)
    pl.semaphore_wait(barrier, len(targets))


class Copies:
    def __init__(self, send_sem, recv_sem):
        self.send_sem, self.recv_sem, self.started = send_sem, recv_sem, {}

    def start(self, name, src, dst, target):
        at = len(self.started)
        copy = pltpu.make_async_remote_copy(
            src_ref=src, dst_ref=dst, send_sem=self.send_sem.at[at], recv_sem=self.recv_sem.at[at],
            device_id=target, device_id_type=MESH)
        copy.start()
        self.started[name] = copy

    def arrived(self, *names):
        for name in names:
            self.started[name].wait_recv()

    def finish(self):
        for copy in self.started.values():
            copy.wait_send()


RY, RYL = 288, 144
RZ, RZL = N - RY, 112
Y_ALL, Y_LO, Y_HI = pl.ds(0, RY), pl.ds(0, RYL), pl.ds(RYL, RY - RYL)
Z_ALL, Z_LO, Z_HI = pl.ds(RY, RZ), pl.ds(RY, RZL), pl.ds(RY + RZL, RZ - RZL)


def dot(a, b):
    return jnp.dot(a, b, preferred_element_type=f32)


def split(a):
    high = a.astype(bf16)
    return high, (a - high.astype(f32)).astype(bf16)


def total(a):
    return jnp.sum(jnp.sum(a, axis=0, keepdims=True), axis=1, keepdims=True)


def roots(stats, keep, kept, outs, d, q, u, hb, h, w, wide, tall):
    both, strip = range(2), 128
    upper, lower, half = pl.ds(0, N // 2), pl.ds(N // 2, N // 2), N // 2
    rows = lax.broadcasted_iota(jnp.int32, (strip, N), 0)
    cols = lax.broadcasted_iota(jnp.int32, (strip, N), 1)
    final = []

    def product(left, right):
        return dot(left[0:half, :], right[...]), dot(left[half:N, :], right[:, half:N])

    def mirror(ref, top, corner):
        ref[upper, :], ref[lower, half:N], ref[lower, 0:half] = top, corner, top[:, half:N].T

    for m in both:
        diagonal = jnp.zeros((strip, strip), f32)
        for at in range(0, N, strip):
            diagonal = diagonal + jnp.where(rows == cols, 1.0, 0.0)[:, 0:strip] * stats[m][at:at + strip, at:at + strip]
        scale = total(diagonal) * (2.0 / N)
        final.append(lax.rsqrt(jnp.sqrt(scale)))
        quarter = 0.25 / scale
        for at in range(0, N, strip):
            here = pl.ds(at, strip)
            eye = jnp.where(rows + at == cols, 1.0, 0.0).astype(f32)
            first = 0.25 * eye - stats[m][here, :] * quarter
            high, rest = split(first)
            d[m, here, :] = high
            h[m, here, :] = eye + first
            hb[m, here, :] = (eye + first).astype(bf16)
            wide[m, here, 0:N], wide[m, here, N:2 * N], wide[m, here, 2 * N:3 * N] = high, high, rest
            for k, value in enumerate((high, rest, high)):
                tall[m, pl.ds(k * N + at, strip), :] = value

    for sweep in range(ITERS):
        if sweep < ITERS - 1:
            for m in both:
                top, corner = product(d.at[m], d.at[m]) if sweep > 0 else product(wide.at[m], tall.at[m])
                w[m, upper, :], w[m, lower, half:N] = top, corner
                mirror(q.at[m], top.astype(bf16), corner.astype(bf16))
        if sweep > 0:
            for m in both:
                top, corner = product(hb.at[m], d.at[m])
                top, corner = h[m, upper, :] + top, h[m, lower, half:N] + corner
                if sweep < ITERS - 1:
                    h[m, upper, :], h[m, lower, half:N] = top, corner
                    mirror(hb.at[m], top.astype(bf16), corner.astype(bf16))
                else:
                    top, corner = (top * final[m]).astype(bf16), (corner * final[m]).astype(bf16)
                    mirror(outs[m], top, corner)
                    outs[m][...] = jnp.where(keep, kept[m][...], outs[m][...])
        if sweep == ITERS - 1:
            break
        for m in both:
            top, corner = product(d.at[m], q.at[m])
            square, square_corner = w[m, upper, :], w[m, lower, half:N]
            mirror(u.at[m], (3.75 * square + top).astype(bf16), (3.75 * square_corner + corner).astype(bf16))
            w[m, upper, :], w[m, lower, half:N] = 2.5 * square + 5.0 * top, 2.5 * square_corner + 5.0 * corner
        for m in both:
            top, corner = product(q.at[m], u.at[m])
            mirror(d.at[m], (w[m, upper, :] + top).astype(bf16), (w[m, lower, half:N] + corner).astype(bf16))


def step_kernel(owner_slot, refresh, partials_hbm, left_stat_hbm, right_stat_hbm, left_root_hbm, right_root_hbm,
                out, left_new, right_new, left_out, right_out,
                partials_a, partials_b, left_stat, right_stat, left_root, right_root, g, update,
                st, ra1, ra2, ra3, rb1, sb, rb2, rb3, acc_a, acc_b, sum_a, send_sem, recv_sem, load_sem, *root_scratch):
    loads_a = [pltpu.make_async_copy(partials_hbm.at[i, A_ALL], partials_a.at[i], load_sem.at[i]) for i in range(SLOTS)]
    loads_b = [pltpu.make_async_copy(partials_hbm.at[i, B_ALL], partials_b.at[i], load_sem.at[SLOTS + 4 + i]) for i in range(SLOTS)]
    stats = [pltpu.make_async_copy(src, dst, load_sem.at[SLOTS + i]) for i, (src, dst) in enumerate((
        (left_stat_hbm, left_stat), (right_stat_hbm, right_stat), (left_root_hbm, left_root), (right_root_hbm, right_root)))]
    for copy in loads_a + loads_b:
        copy.start()
    x, yl, yh, z, c = position()
    dp, ow = lax.axis_index("dp"), lax.axis_index("owner")

    def owner(dz, dy, dc=0):
        return (((yh + dy) % 2) * ZS + (z + dz) % ZS) * 2 + (c + dc) % 2

    xp = (((x + 1) % XS) * 2 + yl, ow)
    xm = (((x + XS - 1) % XS) * 2 + yl, ow)
    yo = (x * 2 + 1 - yl, ow)
    zp, zm = (dp, owner(1, 0)), (dp, owner(3, 0))
    yp, co = (dp, owner(0, 1)), (dp, owner(0, 0, 1))
    greet((xp, xm, yo, zp, zm, yp, co))
    for copy in loads_a:
        copy.wait()
    go = Copies(send_sem, recv_sem)

    def block_of(dx, dy):
        slot = ((x + dx) % XS) * 2 + (yl + dy) % 2
        found = jnp.int32(0)
        for r in range(SLOTS):
            found = jnp.where(owner_slot[r, ow] == slot, jnp.int32(r), found)
        return found

    where = {(dx, dy): block_of(dx, dy) for dx in range(XS) for dy in range(2)}

    def stage(dx, dy, rows):
        st[dx * 2 + dy, rows, :] = (partials_a if rows is A_ALL else partials_b)[where[dx, dy]]

    def own(dx, dy, rows):
        return st.at[dx * 2 + dy, rows]

    def first_a(dy):
        stage(2, dy, A_ALL)
        go.start(("a1p", dy), own(2, dy, A_LO), ra1.at[0, dy], xp)
        go.start(("a1m", dy), own(2, dy, A_HI), ra1.at[1, dy], xm)

    def own_a(dy):
        stage(1, dy, A_ALL)
        go.start(("a2p", dy), own(1, dy, A_HI), ra2.at[0, dy, HI_A], xp)
        stage(3, dy, A_ALL)
        go.start(("a2m", dy), own(3, dy, A_LO), ra2.at[1, dy, LO_A], xm)

    def sum_of_a(dy):
        go.arrived(("a1p", dy), ("a1m", dy))
        acc_a[0, dy] = (st[2 + dy, A_LO, :].astype(f32) + ra1[0, dy].astype(f32)).astype(bf16)
        go.start(("a3p", dy), acc_a.at[0, dy], ra2.at[0, dy, LO_A], xp)
        acc_a[1, dy] = (st[6 + dy, A_HI, :].astype(f32) + ra1[1, dy].astype(f32)).astype(bf16)
        go.start(("a3m", dy), acc_a.at[1, dy], ra2.at[1, dy, HI_A], xm)

    def first_b(dx):
        stage(dx, 1, B_ALL)
        go.start(("b1", dx), own(dx, 1, B_ALL), rb1.at[dx], yo)

    def sum_of_b(dx):
        stage(dx, 0, B_ALL)
        go.arrived(("b1", dx))
        sb[dx] = (st[dx * 2, B_ALL, :].astype(f32) + rb1[dx].astype(f32)).astype(bf16)

    first_a(1)
    for copy in loads_b:
        copy.wait()
    for copy in stats:
        copy.start()
    first_b(2)
    first_a(0)
    own_a(1)
    first_b(1)
    stage(0, 0, A_ALL)
    stage(0, 1, A_ALL)
    sum_of_a(1)
    sum_of_b(2)
    first_b(3)
    own_a(0)
    sum_of_a(0)
    go.start("b2p", sb.at[2, LO_B], rb2.at[0], xp)
    go.start("b2m", sb.at[2, HI_B], rb2.at[1], xm)
    sum_of_b(1)
    first_b(0)
    go.start("b3p", sb.at[1, HI_B], rb3.at[0, HI_B], xp)
    go.arrived(("a2p", 1), ("a2m", 1), ("a3p", 1), ("a3m", 1))
    sum_a[...] = (st[1, A_ALL, :].astype(f32) + ra2[0, 1].astype(f32) + ra2[1, 1].astype(f32)).astype(bf16)
    go.start("a4", sum_a, ra3, yo)
    sum_of_b(3)
    go.start("b3m", sb.at[3, LO_B], rb3.at[1, LO_B], xm)
    go.arrived("b2p", "b2m")
    acc_b[0] = (sb[1, LO_B, :].astype(f32) + rb2[0].astype(f32)).astype(bf16)
    go.start("b4p", acc_b.at[0], rb3.at[0, LO_B], xp)
    acc_b[1] = (sb[3, HI_B, :].astype(f32) + rb2[1].astype(f32)).astype(bf16)
    go.start("b4m", acc_b.at[1], rb3.at[1, HI_B], xm)
    go.arrived(("a2p", 0), ("a2m", 0), ("a3p", 0), ("a3m", 0))
    stage(0, 0, B_ALL)
    go.arrived(("b1", 0))
    go.arrived("a4")
    g[A_ALL, :] = (st[0, A_ALL, :].astype(f32) + ra2[0, 0].astype(f32) + ra2[1, 0].astype(f32)
                       + ra3[...].astype(f32)).astype(bf16)
    go.arrived("b3p", "b3m", "b4p", "b4m")
    g[B_ALL, :] = (st[0, B_ALL, :].astype(f32) + rb1[0].astype(f32) + rb3[0].astype(f32)
                       + rb3[1].astype(f32)).astype(bf16)

    block = ow * SLOTS
    for r in range(SLOTS):
        block = jnp.where(owner_slot[r, ow] == dp, ow * SLOTS + r, block)
    hits = jnp.int32(0)
    for i in range(REFRESH):
        hits = hits + jnp.where(refresh[i] == block, jnp.int32(1), jnp.int32(0))
    for copy in stats:
        copy.wait()
    low = g[...]
    low_t = low.T
    weight = (1.0 - decay_rate) / N
    left_new[...] = decay_rate * left_stat[...] + weight * dot(low, low_t)
    right_new[...] = decay_rate * right_stat[...] + weight * dot(low_t, low)
    roots((left_new, right_new), hits == 0, (left_root, right_root), (left_out, right_out), *root_scratch)
    raw = dot(dot(left_out[...], low).astype(bf16), right_out[...])
    full = low.astype(f32)
    graft = jnp.sqrt(total(full * full) * (1.0 / (N * N))) / jnp.sqrt(total(raw * raw) * (1.0 / (N * N)) + graft_eps)
    update[...] = (raw * graft).astype(bf16)

    def pass_on(name, dz, dy, rows, target):
        piece = out.at[owner(dz, dy), rows]
        go.start(name, piece, piece, target)

    def share(dz, dy, rows, tag):
        pass_on(("core", dz, dy, tag), dz, dy, rows, co)

    def mine(name, rows, target):
        go.start(name, update.at[rows], out.at[owner(0, 0), rows], target)

    mine("yY", Y_ALL, yp)
    mine("zZ+", Z_ALL, zp)
    mine("zZ-", Z_ALL, zm)
    mine("zY+", Y_ALL, zp)
    mine("zY-", Y_ALL, zm)
    mine("yZ", Z_ALL, yp)
    mine("core", pl.ds(0, N), co)
    out[owner(0, 0)] = update[...]

    go.arrived("zZ+")
    pass_on("zZ2+", 3, 0, Z_LO, zp)
    pass_on("yZ-", 3, 0, Z_ALL, yp)
    share(3, 0, Z_ALL, "Z")
    go.arrived("zZ-")
    pass_on("zZ2-", 1, 0, Z_HI, zm)
    pass_on("yZ+", 1, 0, Z_ALL, yp)
    share(1, 0, Z_ALL, "Z")
    go.arrived("yY")
    pass_on("pY+", 0, 1, Y_ALL, zp)
    pass_on("pY-", 0, 1, Y_ALL, zm)
    share(0, 1, Y_ALL, "Y")
    go.arrived("zY+")
    pass_on("zY2+", 3, 0, Y_LO, zp)
    share(3, 0, Y_ALL, "Y")
    go.arrived("zY-")
    pass_on("zY2-", 1, 0, Y_HI, zm)
    share(1, 0, Y_ALL, "Y")
    go.arrived("yZ")
    share(0, 1, Z_ALL, "Z")
    go.arrived("zZ2+", "zZ2-")
    pass_on("yZ2", 2, 0, Z_ALL, yp)
    share(2, 0, Z_ALL, "Z")
    go.arrived("yZ-")
    share(3, 1, Z_ALL, "Z")
    go.arrived("pY+")
    pass_on("pY2+", 3, 1, Y_LO, zp)
    share(3, 1, Y_ALL, "Y")
    go.arrived("pY-")
    pass_on("pY2-", 1, 1, Y_HI, zm)
    share(1, 1, Y_ALL, "Y")
    go.arrived("yZ+")
    share(1, 1, Z_ALL, "Z")
    go.arrived("zY2+", "zY2-")
    share(2, 0, Y_ALL, "Y")
    go.arrived("yZ2")
    share(2, 1, Z_ALL, "Z")
    go.arrived("pY2+", "pY2-")
    share(2, 1, Y_ALL, "Y")
    go.arrived("core", *[name for name in go.started if name[0] == "core" and len(name) == 4 and name != "core"])
    go.finish()


def whole_step(*arrays):
    vmem, smem, hbm = (pl.BlockSpec(memory_space=space) for space in (pltpu.VMEM, pltpu.SMEM, pltpu.HBM))
    like = lambda dtype, *lead: pltpu.VMEM(lead + (N, N), dtype)
    vm = lambda *shape: pltpu.VMEM(shape + (N,), bf16)
    copies = 23 + 33
    return pl.pallas_call(
        step_kernel,
        out_shape=(like(bf16, 16), like(f32), like(f32), like(bf16), like(bf16)),
        in_specs=[smem] * 2 + [hbm] * 5,
        out_specs=[vmem] * 5,
        scratch_shapes=[
            vm(SLOTS, RA), vm(SLOTS, RB), pltpu.VMEM((N, N), f32), pltpu.VMEM((N, N), f32), vm(N), vm(N), vm(N), vm(N),
            vm(SLOTS, N), vm(2, 2, RAH), vm(2, 2, RA), vm(RA), vm(XS, RB), vm(XS, RB), vm(2, RBH), vm(2, RB),
            vm(2, 2, RAH), vm(2, RBH), vm(RA),
            pltpu.SemaphoreType.DMA((copies,)), pltpu.SemaphoreType.DMA((copies,)), pltpu.SemaphoreType.DMA((2 * SLOTS + 4,)),
            *[pltpu.VMEM((2, N, N), dtype) for dtype in (bf16, bf16, bf16, bf16, f32, f32)],
            pltpu.VMEM((2, N, 3 * N), bf16), pltpu.VMEM((2, 3 * N, N), bf16),
        ],
        compiler_params=pltpu.CompilerParams(collective_id=0, has_side_effects=True, vmem_limit_bytes=44 * 2**20),
        name="whole_step",
    )(*arrays)


def write_kernel(*refs):
    count = len(refs) // 2
    sems = refs[-1]
    copies, at = [], 0
    for src, dst in zip(refs[:count], refs[count:-1]):
        parts = [(src.at[i], dst.at[i]) for i in range(src.shape[0])] if len(src.shape) == 3 else [(src, dst)]
        for part in parts:
            copies.append(pltpu.make_async_copy(*part, sems.at[at]))
            copies[-1].start()
            at += 1
    for copy in copies:
        copy.wait()


def write_out(arrays):
    return pl.pallas_call(
        write_kernel,
        out_shape=tuple(jax.ShapeDtypeStruct(a.shape, a.dtype) for a in arrays),
        in_specs=[pl.BlockSpec(memory_space=pltpu.VMEM)] * len(arrays),
        out_specs=[pl.BlockSpec(memory_space=pl.ANY)] * len(arrays),
        scratch_shapes=[pltpu.SemaphoreType.DMA((20,))],
        compiler_params=pltpu.CompilerParams(vmem_limit_bytes=2**20),
        name="write_out",
    )(*arrays)


def body(grad_partials, owner_slot, refresh_blocks, left_stat, right_stat, left_root, right_root):
    results = whole_step(owner_slot.T, refresh_blocks, grad_partials[0], left_stat[0, 0], right_stat[0, 0], left_root[0, 0], right_root[0, 0])
    update, *own = write_out(results)
    return (update[:, None], *(array[None, None] for array in own))


def solution(mesh):
    slots = P("owner", "dp", None, None)
    return jax.shard_map(
        body,
        mesh=mesh,
        in_specs=(P("dp", "owner", None, None), P(), P(), slots, slots, slots, slots),
        out_specs=(P(None, "dp", None, None), slots, slots, slots, slots),
        check_vma=False,
    )
```

```python
import jax
import jax.numpy as jnp
from jax import lax
from jax.experimental import pallas as pl
from jax.experimental.pallas import tpu as pltpu
from jax.sharding import PartitionSpec as P

MESH = pl.DeviceIdType.MESH
f32 = jnp.float32
bf16 = jnp.bfloat16

N = 512
XS, ZS, SLOTS, REFRESH = 4, 4, 8, 32
ITERS = 4
decay_rate = 0.8
graft_eps = 1e-06

RA, RAH = 288, 144
RB, RBH = N - RA, (N - RA) // 2
A_LO, A_HI, A_ALL = pl.ds(0, RAH), pl.ds(RAH, RAH), pl.ds(0, RA)
B_LO, B_HI, B_ALL = pl.ds(RA, RBH), pl.ds(RA + RBH, RBH), pl.ds(RA, RB)
LO_A, HI_A = pl.ds(0, RAH), pl.ds(RAH, RAH)
LO_B, HI_B = pl.ds(0, RBH), pl.ds(RBH, RBH)


def position():
    dp, ow = lax.axis_index("dp"), lax.axis_index("owner")
    return dp // 2, dp % 2, ow // 8, (ow // 2) % 4, ow % 2


def greet(targets):
    barrier = pltpu.get_barrier_semaphore()
    for target in targets:
        pl.semaphore_signal(barrier, inc=1, device_id=target, device_id_type=MESH)
    return lambda: pl.semaphore_wait(barrier, len(targets))


class Copies:
    def __init__(self, send_sem, recv_sem):
        self.send_sem, self.recv_sem, self.started = send_sem, recv_sem, {}

    def start(self, name, src, dst, target):
        at = len(self.started)
        copy = pltpu.make_async_remote_copy(
            src_ref=src, dst_ref=dst, send_sem=self.send_sem.at[at], recv_sem=self.recv_sem.at[at],
            device_id=target, device_id_type=MESH)
        copy.start()
        self.started[name] = copy

    def arrived(self, *names):
        for name in names:
            self.started[name].wait_recv()

    def finish(self):
        for copy in self.started.values():
            copy.wait_send()


RY, RYL = 288, 144
RZ, RZL = N - RY, 112
Y_ALL, Y_LO, Y_HI = pl.ds(0, RY), pl.ds(0, RYL), pl.ds(RYL, RY - RYL)
Z_ALL, Z_LO, Z_HI = pl.ds(RY, RZ), pl.ds(RY, RZL), pl.ds(RY + RZL, RZ - RZL)


def dot(a, b):
    return jnp.dot(a, b, preferred_element_type=f32)


def split(a):
    high = a.astype(bf16)
    return high, (a - high.astype(f32)).astype(bf16)


def total(a):
    return jnp.sum(jnp.sum(a, axis=0, keepdims=True), axis=1, keepdims=True)


def roots(stats, keep, kept, outs, d, q, u, hb, h, w, wide, tall):
    both, strip = range(2), 128
    upper, lower, half = pl.ds(0, N // 2), pl.ds(N // 2, N // 2), N // 2
    rows = lax.broadcasted_iota(jnp.int32, (strip, N), 0)
    cols = lax.broadcasted_iota(jnp.int32, (strip, N), 1)
    final = []

    def product(left, right):
        return dot(left[0:half, :], right[...]), dot(left[half:N, :], right[:, half:N])

    def mirror(ref, top, corner):
        ref[upper, :], ref[lower, half:N], ref[lower, 0:half] = top, corner, top[:, half:N].T

    for m in both:
        diagonal = jnp.zeros((strip, strip), f32)
        for at in range(0, N, strip):
            diagonal = diagonal + jnp.where(rows == cols, 1.0, 0.0)[:, 0:strip] * stats[m][at:at + strip, at:at + strip]
        scale = total(diagonal) * (2.0 / N)
        final.append(lax.rsqrt(jnp.sqrt(scale)))
        quarter = 0.25 / scale
        for at in range(0, N, strip):
            here = pl.ds(at, strip)
            eye = jnp.where(rows + at == cols, 1.0, 0.0).astype(f32)
            first = 0.25 * eye - stats[m][here, :] * quarter
            high, rest = split(first)
            d[m, here, :] = high
            h[m, here, :] = eye + first
            hb[m, here, :] = (eye + first).astype(bf16)
            wide[m, here, 0:N], wide[m, here, N:2 * N], wide[m, here, 2 * N:3 * N] = high, high, rest
            for k, value in enumerate((high, rest, high)):
                tall[m, pl.ds(k * N + at, strip), :] = value

    for sweep in range(ITERS):
        if sweep < ITERS - 1:
            for m in both:
                top, corner = product(d.at[m], d.at[m]) if sweep > 0 else product(wide.at[m], tall.at[m])
                w[m, upper, :], w[m, lower, half:N] = top, corner
                (top, top_rest), (corner, corner_rest) = split(top), split(corner)
                mirror(q.at[m], top, corner)
                if sweep == 0:
                    mirror(tall.at[m, pl.ds(0, N)], top, corner)
                    mirror(tall.at[m, pl.ds(N, N)], top_rest, corner_rest)
                    mirror(tall.at[m, pl.ds(2 * N, N)], top, corner)
        if sweep > 0:
            for m in both:
                top, corner = product(hb.at[m], d.at[m])
                top, corner = h[m, upper, :] + top, h[m, lower, half:N] + corner
                if sweep < ITERS - 1:
                    h[m, upper, :], h[m, lower, half:N] = top, corner
                    mirror(hb.at[m], top.astype(bf16), corner.astype(bf16))
                else:
                    top, corner = (top * final[m]).astype(bf16), (corner * final[m]).astype(bf16)
                    mirror(outs[m], jnp.where(keep, kept[m][upper, :], top), jnp.where(keep, kept[m][lower, half:N], corner))
                    outs[m][lower, 0:half] = jnp.where(keep, kept[m][lower, 0:half], outs[m][lower, 0:half])
        if sweep == ITERS - 1:
            break
        for m in both:
            top, corner = product(d.at[m], q.at[m]) if sweep > 0 else product(wide.at[m], tall.at[m])
            square, square_corner = w[m, upper, :], w[m, lower, half:N]
            mirror(u.at[m], (3.75 * square + top).astype(bf16), (3.75 * square_corner + corner).astype(bf16))
            w[m, upper, :], w[m, lower, half:N] = 2.5 * square + 5.0 * top, 2.5 * square_corner + 5.0 * corner
        for m in both:
            top, corner = product(q.at[m], u.at[m])
            mirror(d.at[m], (w[m, upper, :] + top).astype(bf16), (w[m, lower, half:N] + corner).astype(bf16))


def step_kernel(owner_slot, refresh, partials_hbm, left_stat_hbm, right_stat_hbm, left_root_hbm, right_root_hbm,
                out, left_new, right_new, left_out, right_out,
                partials_a, partials_b, left_stat, right_stat, left_root, right_root, g, update,
                st, ra1, ra2, ra3, rb1, sb, rb2, rb3, acc_a, acc_b, sum_a, send_sem, recv_sem, load_sem, *root_scratch):
    x, yl, yh, z, c = position()
    dp, ow = lax.axis_index("dp"), lax.axis_index("owner")

    def owner(dz, dy, dc=0):
        return (((yh + dy) % 2) * ZS + (z + dz) % ZS) * 2 + (c + dc) % 2

    xp = (((x + 1) % XS) * 2 + yl, ow)
    xm = (((x + XS - 1) % XS) * 2 + yl, ow)
    yo = (x * 2 + 1 - yl, ow)
    zp, zm = (dp, owner(1, 0)), (dp, owner(3, 0))
    yp, co = (dp, owner(0, 1)), (dp, owner(0, 0, 1))
    met = greet((xp, xm, yo, zp, zm, yp, co))
    loads_a = [pltpu.make_async_copy(partials_hbm.at[i, A_ALL], partials_a.at[i], load_sem.at[i]) for i in range(SLOTS)]
    loads_b = [pltpu.make_async_copy(partials_hbm.at[i, B_ALL], partials_b.at[i], load_sem.at[SLOTS + 4 + i]) for i in range(SLOTS)]
    stats = [pltpu.make_async_copy(src, dst, load_sem.at[SLOTS + i]) for i, (src, dst) in enumerate((
        (left_stat_hbm, left_stat), (right_stat_hbm, right_stat), (left_root_hbm, left_root), (right_root_hbm, right_root)))]
    for copy in loads_a + loads_b:
        copy.start()
    for copy in loads_a:
        copy.wait()
    go = Copies(send_sem, recv_sem)

    def block_of(dx, dy):
        slot = ((x + dx) % XS) * 2 + (yl + dy) % 2
        found = jnp.int32(0)
        for r in range(SLOTS):
            found = jnp.where(owner_slot[r, ow] == slot, jnp.int32(r), found)
        return found

    where = {(dx, dy): block_of(dx, dy) for dx in range(XS) for dy in range(2)}

    def stage(dx, dy, rows):
        st[dx * 2 + dy, rows, :] = (partials_a if rows is A_ALL else partials_b)[where[dx, dy]]

    def own(dx, dy, rows):
        return st.at[dx * 2 + dy, rows]

    def first_a(dy):
        go.start(("a1p", dy), own(2, dy, A_LO), ra1.at[0, dy], xp)
        go.start(("a1m", dy), own(2, dy, A_HI), ra1.at[1, dy], xm)

    def own_a(dy):
        stage(1, dy, A_ALL)
        go.start(("a2p", dy), own(1, dy, A_HI), ra2.at[0, dy, HI_A], xp)
        stage(3, dy, A_ALL)
        go.start(("a2m", dy), own(3, dy, A_LO), ra2.at[1, dy, LO_A], xm)

    def sum_of_a(dy):
        go.arrived(("a1p", dy), ("a1m", dy))
        acc_a[0, dy] = (st[2 + dy, A_LO, :].astype(f32) + ra1[0, dy].astype(f32)).astype(bf16)
        go.start(("a3p", dy), acc_a.at[0, dy], ra2.at[0, dy, LO_A], xp)
        acc_a[1, dy] = (st[6 + dy, A_HI, :].astype(f32) + ra1[1, dy].astype(f32)).astype(bf16)
        go.start(("a3m", dy), acc_a.at[1, dy], ra2.at[1, dy, HI_A], xm)

    def first_b(dx):
        stage(dx, 1, B_ALL)
        go.start(("b1", dx), own(dx, 1, B_ALL), rb1.at[dx], yo)

    def sum_of_b(dx):
        stage(dx, 0, B_ALL)
        go.arrived(("b1", dx))
        sb[dx] = (st[dx * 2, B_ALL, :].astype(f32) + rb1[dx].astype(f32)).astype(bf16)

    stage(2, 1, A_ALL)
    met()
    first_a(1)
    stage(2, 0, A_ALL)
    for copy in loads_b:
        copy.wait()
    for copy in stats:
        copy.start()
    first_b(2)
    first_a(0)
    own_a(1)
    first_b(1)
    stage(0, 0, A_ALL)
    stage(0, 1, A_ALL)
    sum_of_a(1)
    sum_of_b(2)
    first_b(3)
    own_a(0)
    sum_of_a(0)
    go.start("b2p", sb.at[2, LO_B], rb2.at[0], xp)
    go.start("b2m", sb.at[2, HI_B], rb2.at[1], xm)
    sum_of_b(1)
    first_b(0)
    go.start("b3p", sb.at[1, HI_B], rb3.at[0, HI_B], xp)
    go.arrived(("a2p", 1), ("a2m", 1), ("a3p", 1), ("a3m", 1))
    sum_a[...] = (st[1, A_ALL, :].astype(f32) + ra2[0, 1].astype(f32) + ra2[1, 1].astype(f32)).astype(bf16)
    go.start("a4", sum_a, ra3, yo)
    sum_of_b(3)
    go.start("b3m", sb.at[3, LO_B], rb3.at[1, LO_B], xm)
    go.arrived("b2p", "b2m")
    acc_b[0] = (sb[1, LO_B, :].astype(f32) + rb2[0].astype(f32)).astype(bf16)
    go.start("b4p", acc_b.at[0], rb3.at[0, LO_B], xp)
    acc_b[1] = (sb[3, HI_B, :].astype(f32) + rb2[1].astype(f32)).astype(bf16)
    go.start("b4m", acc_b.at[1], rb3.at[1, HI_B], xm)
    go.arrived(("a2p", 0), ("a2m", 0), ("a3p", 0), ("a3m", 0))
    stage(0, 0, B_ALL)
    go.arrived(("b1", 0))
    go.arrived("a4")
    g[A_ALL, :] = (st[0, A_ALL, :].astype(f32) + ra2[0, 0].astype(f32) + ra2[1, 0].astype(f32)
                       + ra3[...].astype(f32)).astype(bf16)
    go.arrived("b3p", "b3m", "b4p", "b4m")
    g[B_ALL, :] = (st[0, B_ALL, :].astype(f32) + rb1[0].astype(f32) + rb3[0].astype(f32)
                       + rb3[1].astype(f32)).astype(bf16)

    block = ow * SLOTS
    for r in range(SLOTS):
        block = jnp.where(owner_slot[r, ow] == dp, ow * SLOTS + r, block)
    hits = jnp.int32(0)
    for i in range(REFRESH):
        hits = hits + jnp.where(refresh[i] == block, jnp.int32(1), jnp.int32(0))
    for copy in stats:
        copy.wait()
    low = g[...]
    low_t = low.T
    weight = (1.0 - decay_rate) / N
    left_new[...] = decay_rate * left_stat[...] + weight * dot(low, low_t)
    right_new[...] = decay_rate * right_stat[...] + weight * dot(low_t, low)
    roots((left_new, right_new), hits == 0, (left_root, right_root), (left_out, right_out), *root_scratch)
    raw = dot(dot(left_out[...], low).astype(bf16), right_out[...])
    full = low.astype(f32)
    graft = jnp.sqrt(total(full * full) * (1.0 / (N * N))) / jnp.sqrt(total(raw * raw) * (1.0 / (N * N)) + graft_eps)
    update[...] = (raw * graft).astype(bf16)

    def pass_on(name, dz, dy, rows, target):
        piece = out.at[owner(dz, dy), rows]
        go.start(name, piece, piece, target)

    def share(dz, dy, rows, tag):
        pass_on(("core", dz, dy, tag), dz, dy, rows, co)

    def mine(name, rows, target):
        go.start(name, update.at[rows], out.at[owner(0, 0), rows], target)

    mine("yY", Y_ALL, yp)
    mine("zZ+", Z_ALL, zp)
    mine("zZ-", Z_ALL, zm)
    mine("zY+", Y_ALL, zp)
    mine("zY-", Y_ALL, zm)
    mine("yZ", Z_ALL, yp)
    out[owner(0, 0)] = update[...]

    go.arrived("zZ+")
    pass_on("zZ2+", 3, 0, Z_LO, zp)
    pass_on("yZ-", 3, 0, Z_ALL, yp)
    share(3, 0, Z_ALL, "Z")
    go.arrived("zZ-")
    pass_on("zZ2-", 1, 0, Z_HI, zm)
    pass_on("yZ+", 1, 0, Z_ALL, yp)
    share(1, 0, Z_ALL, "Z")
    mine("core", pl.ds(0, N), co)
    go.arrived("yY")
    pass_on("pY+", 0, 1, Y_ALL, zp)
    pass_on("pY-", 0, 1, Y_ALL, zm)
    share(0, 1, Y_ALL, "Y")
    go.arrived("zY+")
    pass_on("zY2+", 3, 0, Y_LO, zp)
    share(3, 0, Y_ALL, "Y")
    go.arrived("zY-")
    pass_on("zY2-", 1, 0, Y_HI, zm)
    share(1, 0, Y_ALL, "Y")
    go.arrived("yZ")
    share(0, 1, Z_ALL, "Z")
    go.arrived("zZ2+", "zZ2-")
    pass_on("yZ2", 2, 0, Z_ALL, yp)
    share(2, 0, Z_ALL, "Z")
    go.arrived("yZ-")
    share(3, 1, Z_ALL, "Z")
    go.arrived("pY+")
    pass_on("pY2+", 3, 1, Y_LO, zp)
    share(3, 1, Y_ALL, "Y")
    go.arrived("pY-")
    pass_on("pY2-", 1, 1, Y_HI, zm)
    share(1, 1, Y_ALL, "Y")
    go.arrived("yZ+")
    share(1, 1, Z_ALL, "Z")
    go.arrived("zY2+", "zY2-")
    share(2, 0, Y_ALL, "Y")
    go.arrived("yZ2")
    share(2, 1, Z_ALL, "Z")
    go.arrived("pY2+", "pY2-")
    share(2, 1, Y_ALL, "Y")
    go.arrived("core", *[name for name in go.started if name[0] == "core" and len(name) == 4 and name != "core"])
    go.finish()


def whole_step(*arrays):
    vmem, smem, hbm = (pl.BlockSpec(memory_space=space) for space in (pltpu.VMEM, pltpu.SMEM, pltpu.HBM))
    like = lambda dtype, *lead: pltpu.VMEM(lead + (N, N), dtype)
    vm = lambda *shape: pltpu.VMEM(shape + (N,), bf16)
    copies = 23 + 33
    return pl.pallas_call(
        step_kernel,
        out_shape=(like(bf16, 16), like(f32), like(f32), like(bf16), like(bf16)),
        in_specs=[smem] * 2 + [hbm] * 5,
        out_specs=[vmem] * 5,
        scratch_shapes=[
            vm(SLOTS, RA), vm(SLOTS, RB), pltpu.VMEM((N, N), f32), pltpu.VMEM((N, N), f32), vm(N), vm(N), vm(N), vm(N),
            vm(SLOTS, N), vm(2, 2, RAH), vm(2, 2, RA), vm(RA), vm(XS, RB), vm(XS, RB), vm(2, RBH), vm(2, RB),
            vm(2, 2, RAH), vm(2, RBH), vm(RA),
            pltpu.SemaphoreType.DMA((copies,)), pltpu.SemaphoreType.DMA((copies,)), pltpu.SemaphoreType.DMA((2 * SLOTS + 4,)),
            *[pltpu.VMEM((2, N, N), dtype) for dtype in (bf16, bf16, bf16, bf16, f32, f32)],
            pltpu.VMEM((2, N, 3 * N), bf16), pltpu.VMEM((2, 3 * N, N), bf16),
        ],
        compiler_params=pltpu.CompilerParams(collective_id=0, has_side_effects=True, vmem_limit_bytes=44 * 2**20),
        name="whole_step",
    )(*arrays)


def write_kernel(*refs):
    count = len(refs) // 2
    sems = refs[-1]
    copies, at = [], 0
    for src, dst in zip(refs[:count], refs[count:-1]):
        parts = [(src.at[i], dst.at[i]) for i in range(src.shape[0])] if len(src.shape) == 3 else [(src, dst)]
        for part in parts:
            copies.append(pltpu.make_async_copy(*part, sems.at[at]))
            copies[-1].start()
            at += 1
    for copy in copies:
        copy.wait()


def write_out(arrays):
    return pl.pallas_call(
        write_kernel,
        out_shape=tuple(jax.ShapeDtypeStruct(a.shape, a.dtype) for a in arrays),
        in_specs=[pl.BlockSpec(memory_space=pltpu.VMEM)] * len(arrays),
        out_specs=[pl.BlockSpec(memory_space=pl.ANY)] * len(arrays),
        scratch_shapes=[pltpu.SemaphoreType.DMA((20,))],
        compiler_params=pltpu.CompilerParams(vmem_limit_bytes=2**20),
        name="write_out",
    )(*arrays)


def body(grad_partials, owner_slot, refresh_blocks, left_stat, right_stat, left_root, right_root):
    results = whole_step(owner_slot.T, refresh_blocks, grad_partials[0], left_stat[0, 0], right_stat[0, 0], left_root[0, 0], right_root[0, 0])
    update, *own = write_out(results)
    return (update[:, None], *(array[None, None] for array in own))


def solution(mesh):
    slots = P("owner", "dp", None, None)
    return jax.shard_map(
        body,
        mesh=mesh,
        in_specs=(P("dp", "owner", None, None), P(), P(), slots, slots, slots, slots),
        out_specs=(P(None, "dp", None, None), slots, slots, slots, slots),
        check_vma=False,
    )
```

```python
import jax
import jax.numpy as jnp
from jax import lax
from jax.experimental import pallas as pl
from jax.experimental.pallas import tpu as pltpu
from jax.sharding import PartitionSpec as P

MESH = pl.DeviceIdType.MESH
f32 = jnp.float32
bf16 = jnp.bfloat16

N = 512
XS, ZS, SLOTS, REFRESH = 4, 4, 8, 32
ITERS = 4
decay_rate = 0.8
graft_eps = 1e-06

RA, RAH = 288, 144
RB, RBH = N - RA, (N - RA) // 2
A_LO, A_HI, A_ALL = pl.ds(0, RAH), pl.ds(RAH, RAH), pl.ds(0, RA)
B_LO, B_HI, B_ALL = pl.ds(RA, RBH), pl.ds(RA + RBH, RBH), pl.ds(RA, RB)
LO_A, HI_A = pl.ds(0, RAH), pl.ds(RAH, RAH)
LO_B, HI_B = pl.ds(0, RBH), pl.ds(RBH, RBH)


def position():
    dp, ow = lax.axis_index("dp"), lax.axis_index("owner")
    return dp // 2, dp % 2, ow // 8, (ow // 2) % 4, ow % 2


def greet(targets):
    barrier = pltpu.get_barrier_semaphore()
    for target in targets:
        pl.semaphore_signal(barrier, inc=1, device_id=target, device_id_type=MESH)
    return lambda: pl.semaphore_wait(barrier, len(targets))


class Copies:
    def __init__(self, send_sem, recv_sem):
        self.send_sem, self.recv_sem, self.started = send_sem, recv_sem, {}

    def start(self, name, src, dst, target):
        at = len(self.started)
        copy = pltpu.make_async_remote_copy(
            src_ref=src, dst_ref=dst, send_sem=self.send_sem.at[at], recv_sem=self.recv_sem.at[at],
            device_id=target, device_id_type=MESH)
        copy.start()
        self.started[name] = copy

    def arrived(self, *names):
        for name in names:
            self.started[name].wait_recv()

    def finish(self):
        for copy in self.started.values():
            copy.wait_send()


RY, RYL = 288, 144
RZ, RZL = N - RY, 112
Y_ALL, Y_LO, Y_HI = pl.ds(0, RY), pl.ds(0, RYL), pl.ds(RYL, RY - RYL)
Z_ALL, Z_LO, Z_HI = pl.ds(RY, RZ), pl.ds(RY, RZL), pl.ds(RY + RZL, RZ - RZL)


def dot(a, b):
    return jnp.dot(a, b, preferred_element_type=f32)


def split(a):
    high = a.astype(bf16)
    return high, (a - high.astype(f32)).astype(bf16)


def total(a):
    return jnp.sum(jnp.sum(a, axis=0, keepdims=True), axis=1, keepdims=True)


def roots(stats, keep, kept, outs, d, q, u, hb, h, w, wide, tall):
    both, strip = range(2), 128
    upper, lower, half = pl.ds(0, N // 2), pl.ds(N // 2, N // 2), N // 2
    rows = lax.broadcasted_iota(jnp.int32, (strip, N), 0)
    cols = lax.broadcasted_iota(jnp.int32, (strip, N), 1)
    final = []

    def product(left, right):
        return dot(left[0:half, :], right[...]), dot(left[half:N, :], right[:, half:N])

    def mirror(ref, top, corner):
        ref[upper, :], ref[lower, half:N], ref[lower, 0:half] = top, corner, top[:, half:N].T

    for m in both:
        diagonal = jnp.zeros((strip, strip), f32)
        for at in range(0, N, strip):
            diagonal = diagonal + jnp.where(rows == cols, 1.0, 0.0)[:, 0:strip] * stats[m][at:at + strip, at:at + strip]
        scale = total(diagonal) * (2.0 / N)
        final.append(lax.rsqrt(jnp.sqrt(scale)))
        quarter = 0.25 / scale
        for at in range(0, N, strip):
            here = pl.ds(at, strip)
            eye = jnp.where(rows + at == cols, 1.0, 0.0).astype(f32)
            first = 0.25 * eye - stats[m][here, :] * quarter
            high, rest = split(first)
            d[m, here, :] = high
            h[m, here, :] = eye + first
            hb[m, here, :] = (eye + first).astype(bf16)
            wide[m, here, 0:N], wide[m, here, N:2 * N], wide[m, here, 2 * N:3 * N] = high, high, rest
            for k, value in enumerate((high, rest, high)):
                tall[m, pl.ds(k * N + at, strip), :] = value

    for sweep in range(ITERS):
        if sweep < ITERS - 1:
            for m in both:
                top, corner = product(d.at[m], d.at[m]) if sweep > 0 else product(wide.at[m], tall.at[m])
                w[m, upper, :], w[m, lower, half:N] = top, corner
                (top, top_rest), (corner, corner_rest) = split(top), split(corner)
                if sweep > 0:
                    mirror(q.at[m], top, corner)
                else:
                    mirror(tall.at[m, pl.ds(0, N)], top, corner)
                    mirror(tall.at[m, pl.ds(N, N)], top_rest, corner_rest)
                    mirror(tall.at[m, pl.ds(2 * N, N)], top, corner)
        if sweep > 0:
            for m in both:
                top, corner = product(hb.at[m], d.at[m])
                top, corner = h[m, upper, :] + top, h[m, lower, half:N] + corner
                if sweep < ITERS - 1:
                    h[m, upper, :], h[m, lower, half:N] = top, corner
                    mirror(hb.at[m], top.astype(bf16), corner.astype(bf16))
                else:
                    top, corner = (top * final[m]).astype(bf16), (corner * final[m]).astype(bf16)
                    mirror(outs[m], jnp.where(keep, kept[m][upper, :], top), jnp.where(keep, kept[m][lower, half:N], corner))
                    outs[m][lower, 0:half] = jnp.where(keep, kept[m][lower, 0:half], outs[m][lower, 0:half])
        if sweep == ITERS - 1:
            break
        for m in both:
            top, corner = product(d.at[m], q.at[m]) if sweep > 0 else product(wide.at[m], tall.at[m])
            square, square_corner = w[m, upper, :], w[m, lower, half:N]
            mirror(u.at[m], (3.75 * square + top).astype(bf16), (3.75 * square_corner + corner).astype(bf16))
            w[m, upper, :], w[m, lower, half:N] = 2.5 * square + 5.0 * top, 2.5 * square_corner + 5.0 * corner
        for m in both:
            top, corner = product(q.at[m] if sweep > 0 else tall.at[m, pl.ds(0, N)], u.at[m])
            mirror(d.at[m], (w[m, upper, :] + top).astype(bf16), (w[m, lower, half:N] + corner).astype(bf16))


def step_kernel(owner_slot, refresh, partials_hbm, left_stat_hbm, right_stat_hbm, left_root_hbm, right_root_hbm,
                out, left_new, right_new, left_out, right_out,
                partials_a, partials_b, left_stat, right_stat, left_root, right_root, g, update,
                st, ra1, ra2, ra3, rb1, sb, rb2, rb3, acc_a, acc_b, sum_a, send_sem, recv_sem, load_sem, *root_scratch):
    x, yl, yh, z, c = position()
    dp, ow = lax.axis_index("dp"), lax.axis_index("owner")

    def owner(dz, dy, dc=0):
        return (((yh + dy) % 2) * ZS + (z + dz) % ZS) * 2 + (c + dc) % 2

    xp = (((x + 1) % XS) * 2 + yl, ow)
    xm = (((x + XS - 1) % XS) * 2 + yl, ow)
    yo = (x * 2 + 1 - yl, ow)
    zp, zm = (dp, owner(1, 0)), (dp, owner(3, 0))
    yp, co = (dp, owner(0, 1)), (dp, owner(0, 0, 1))
    met = greet((xp, xm, yo, zp, zm, yp, co))
    loads_a = [pltpu.make_async_copy(partials_hbm.at[i, A_ALL], partials_a.at[i], load_sem.at[i]) for i in range(SLOTS)]
    loads_b = [pltpu.make_async_copy(partials_hbm.at[i, B_ALL], partials_b.at[i], load_sem.at[SLOTS + 4 + i]) for i in range(SLOTS)]
    stats = [pltpu.make_async_copy(src, dst, load_sem.at[SLOTS + i]) for i, (src, dst) in enumerate((
        (left_stat_hbm, left_stat), (right_stat_hbm, right_stat), (left_root_hbm, left_root), (right_root_hbm, right_root)))]
    for copy in loads_a + loads_b:
        copy.start()
    for copy in loads_a:
        copy.wait()
    go = Copies(send_sem, recv_sem)

    def block_of(dx, dy):
        slot = ((x + dx) % XS) * 2 + (yl + dy) % 2
        found = jnp.int32(0)
        for r in range(SLOTS):
            found = jnp.where(owner_slot[r, ow] == slot, jnp.int32(r), found)
        return found

    where = {(dx, dy): block_of(dx, dy) for dx in range(XS) for dy in range(2)}

    def stage(dx, dy, rows):
        st[dx * 2 + dy, rows, :] = (partials_a if rows is A_ALL else partials_b)[where[dx, dy]]

    def own(dx, dy, rows):
        return st.at[dx * 2 + dy, rows]

    def first_a(dy):
        go.start(("a1p", dy), own(2, dy, A_LO), ra1.at[0, dy], xp)
        go.start(("a1m", dy), own(2, dy, A_HI), ra1.at[1, dy], xm)

    def own_a(dy):
        stage(1, dy, A_ALL)
        go.start(("a2p", dy), own(1, dy, A_HI), ra2.at[0, dy, HI_A], xp)
        stage(3, dy, A_ALL)
        go.start(("a2m", dy), own(3, dy, A_LO), ra2.at[1, dy, LO_A], xm)

    def sum_of_a(dy):
        go.arrived(("a1p", dy), ("a1m", dy))
        acc_a[0, dy] = (st[2 + dy, A_LO, :].astype(f32) + ra1[0, dy].astype(f32)).astype(bf16)
        go.start(("a3p", dy), acc_a.at[0, dy], ra2.at[0, dy, LO_A], xp)
        acc_a[1, dy] = (st[6 + dy, A_HI, :].astype(f32) + ra1[1, dy].astype(f32)).astype(bf16)
        go.start(("a3m", dy), acc_a.at[1, dy], ra2.at[1, dy, HI_A], xm)

    def first_b(dx):
        stage(dx, 1, B_ALL)
        go.start(("b1", dx), own(dx, 1, B_ALL), rb1.at[dx], yo)

    def sum_of_b(dx):
        stage(dx, 0, B_ALL)
        go.arrived(("b1", dx))
        sb[dx] = (st[dx * 2, B_ALL, :].astype(f32) + rb1[dx].astype(f32)).astype(bf16)

    stage(2, 1, A_ALL)
    met()
    first_a(1)
    stage(2, 0, A_ALL)
    for copy in loads_b:
        copy.wait()
    for copy in stats:
        copy.start()
    first_b(2)
    first_a(0)
    own_a(1)
    first_b(1)
    stage(0, 0, A_ALL)
    stage(0, 1, A_ALL)
    sum_of_a(1)
    sum_of_b(2)
    first_b(3)
    own_a(0)
    sum_of_a(0)
    go.start("b2p", sb.at[2, LO_B], rb2.at[0], xp)
    go.start("b2m", sb.at[2, HI_B], rb2.at[1], xm)
    sum_of_b(1)
    first_b(0)
    go.start("b3p", sb.at[1, HI_B], rb3.at[0, HI_B], xp)
    go.arrived(("a2p", 1), ("a2m", 1), ("a3p", 1), ("a3m", 1))
    sum_a[...] = (st[1, A_ALL, :].astype(f32) + ra2[0, 1].astype(f32) + ra2[1, 1].astype(f32)).astype(bf16)
    go.start("a4", sum_a, ra3, yo)
    sum_of_b(3)
    go.start("b3m", sb.at[3, LO_B], rb3.at[1, LO_B], xm)
    go.arrived("b2p", "b2m")
    acc_b[0] = (sb[1, LO_B, :].astype(f32) + rb2[0].astype(f32)).astype(bf16)
    go.start("b4p", acc_b.at[0], rb3.at[0, LO_B], xp)
    acc_b[1] = (sb[3, HI_B, :].astype(f32) + rb2[1].astype(f32)).astype(bf16)
    go.start("b4m", acc_b.at[1], rb3.at[1, HI_B], xm)
    go.arrived(("a2p", 0), ("a2m", 0), ("a3p", 0), ("a3m", 0))
    stage(0, 0, B_ALL)
    go.arrived(("b1", 0))
    go.arrived("a4")
    g[A_ALL, :] = (st[0, A_ALL, :].astype(f32) + ra2[0, 0].astype(f32) + ra2[1, 0].astype(f32)
                       + ra3[...].astype(f32)).astype(bf16)
    go.arrived("b3p", "b3m", "b4p", "b4m")
    g[B_ALL, :] = (st[0, B_ALL, :].astype(f32) + rb1[0].astype(f32) + rb3[0].astype(f32)
                       + rb3[1].astype(f32)).astype(bf16)

    block = ow * SLOTS
    for r in range(SLOTS):
        block = jnp.where(owner_slot[r, ow] == dp, ow * SLOTS + r, block)
    hits = jnp.int32(0)
    for i in range(REFRESH):
        hits = hits + jnp.where(refresh[i] == block, jnp.int32(1), jnp.int32(0))
    for copy in stats:
        copy.wait()
    low = g[...]
    low_t = low.T
    weight = (1.0 - decay_rate) / N
    left_new[...] = decay_rate * left_stat[...] + weight * dot(low, low_t)
    right_new[...] = decay_rate * right_stat[...] + weight * dot(low_t, low)
    roots((left_new, right_new), hits == 0, (left_root, right_root), (left_out, right_out), *root_scratch)
    raw = dot(dot(left_out[...], low).astype(bf16), right_out[...])
    full = low.astype(f32)
    graft = jnp.sqrt(total(full * full) * (1.0 / (N * N))) / jnp.sqrt(total(raw * raw) * (1.0 / (N * N)) + graft_eps)
    update[Y_ALL, :] = (raw[0:RY] * graft).astype(bf16)

    def pass_on(name, dz, dy, rows, target):
        piece = out.at[owner(dz, dy), rows]
        go.start(name, piece, piece, target)

    def share(dz, dy, rows, tag):
        pass_on(("core", dz, dy, tag), dz, dy, rows, co)

    def mine(name, rows, target):
        go.start(name, update.at[rows], out.at[owner(0, 0), rows], target)

    mine("yY", Y_ALL, yp)
    update[Z_ALL, :] = (raw[RY:N] * graft).astype(bf16)
    mine("zZ+", Z_ALL, zp)
    mine("zZ-", Z_ALL, zm)
    mine("zY+", Y_ALL, zp)
    mine("zY-", Y_ALL, zm)
    mine("yZ", Z_ALL, yp)
    out[owner(0, 0)] = update[...]

    go.arrived("zZ+")
    pass_on("zZ2+", 3, 0, Z_LO, zp)
    pass_on("yZ-", 3, 0, Z_ALL, yp)
    share(3, 0, Z_ALL, "Z")
    go.arrived("zZ-")
    pass_on("zZ2-", 1, 0, Z_HI, zm)
    pass_on("yZ+", 1, 0, Z_ALL, yp)
    share(1, 0, Z_ALL, "Z")
    mine("core", pl.ds(0, N), co)
    go.arrived("yY")
    pass_on("pY+", 0, 1, Y_ALL, zp)
    pass_on("pY-", 0, 1, Y_ALL, zm)
    share(0, 1, Y_ALL, "Y")
    go.arrived("zY+")
    pass_on("zY2+", 3, 0, Y_LO, zp)
    share(3, 0, Y_ALL, "Y")
    go.arrived("zY-")
    pass_on("zY2-", 1, 0, Y_HI, zm)
    share(1, 0, Y_ALL, "Y")
    go.arrived("yZ")
    share(0, 1, Z_ALL, "Z")
    go.arrived("zZ2+", "zZ2-")
    pass_on("yZ2", 2, 0, Z_ALL, yp)
    share(2, 0, Z_ALL, "Z")
    go.arrived("yZ-")
    share(3, 1, Z_ALL, "Z")
    go.arrived("pY+")
    pass_on("pY2+", 3, 1, Y_LO, zp)
    share(3, 1, Y_ALL, "Y")
    go.arrived("pY-")
    pass_on("pY2-", 1, 1, Y_HI, zm)
    share(1, 1, Y_ALL, "Y")
    go.arrived("yZ+")
    share(1, 1, Z_ALL, "Z")
    go.arrived("zY2+", "zY2-")
    share(2, 0, Y_ALL, "Y")
    go.arrived("yZ2")
    share(2, 1, Z_ALL, "Z")
    go.arrived("pY2+", "pY2-")
    share(2, 1, Y_ALL, "Y")
    go.arrived("core", *[name for name in go.started if name[0] == "core" and len(name) == 4 and name != "core"])
    go.finish()


def whole_step(*arrays):
    vmem, smem, hbm = (pl.BlockSpec(memory_space=space) for space in (pltpu.VMEM, pltpu.SMEM, pltpu.HBM))
    like = lambda dtype, *lead: pltpu.VMEM(lead + (N, N), dtype)
    vm = lambda *shape: pltpu.VMEM(shape + (N,), bf16)
    copies = 23 + 33
    return pl.pallas_call(
        step_kernel,
        out_shape=(like(bf16, 16), like(f32), like(f32), like(bf16), like(bf16)),
        in_specs=[smem] * 2 + [hbm] * 5,
        out_specs=[vmem] * 5,
        scratch_shapes=[
            vm(SLOTS, RA), vm(SLOTS, RB), pltpu.VMEM((N, N), f32), pltpu.VMEM((N, N), f32), vm(N), vm(N), vm(N), vm(N),
            vm(SLOTS, N), vm(2, 2, RAH), vm(2, 2, RA), vm(RA), vm(XS, RB), vm(XS, RB), vm(2, RBH), vm(2, RB),
            vm(2, 2, RAH), vm(2, RBH), vm(RA),
            pltpu.SemaphoreType.DMA((copies,)), pltpu.SemaphoreType.DMA((copies,)), pltpu.SemaphoreType.DMA((2 * SLOTS + 4,)),
            *[pltpu.VMEM((2, N, N), dtype) for dtype in (bf16, bf16, bf16, bf16, f32, f32)],
            pltpu.VMEM((2, N, 3 * N), bf16), pltpu.VMEM((2, 3 * N, N), bf16),
        ],
        compiler_params=pltpu.CompilerParams(collective_id=0, has_side_effects=True, vmem_limit_bytes=44 * 2**20),
        name="whole_step",
    )(*arrays)


def write_kernel(*refs):
    count = len(refs) // 2
    sems = refs[-1]
    copies, at = [], 0
    for src, dst in zip(refs[:count], refs[count:-1]):
        parts = [(src.at[i], dst.at[i]) for i in range(src.shape[0])] if len(src.shape) == 3 else [(src, dst)]
        for part in parts:
            copies.append(pltpu.make_async_copy(*part, sems.at[at]))
            copies[-1].start()
            at += 1
    for copy in copies:
        copy.wait()


def write_out(arrays):
    return pl.pallas_call(
        write_kernel,
        out_shape=tuple(jax.ShapeDtypeStruct(a.shape, a.dtype) for a in arrays),
        in_specs=[pl.BlockSpec(memory_space=pltpu.VMEM)] * len(arrays),
        out_specs=[pl.BlockSpec(memory_space=pl.ANY)] * len(arrays),
        scratch_shapes=[pltpu.SemaphoreType.DMA((20,))],
        compiler_params=pltpu.CompilerParams(vmem_limit_bytes=2**20),
        name="write_out",
    )(*arrays)


def body(grad_partials, owner_slot, refresh_blocks, left_stat, right_stat, left_root, right_root):
    results = whole_step(owner_slot.T, refresh_blocks, grad_partials[0], left_stat[0, 0], right_stat[0, 0], left_root[0, 0], right_root[0, 0])
    update, *own = write_out(results)
    return (update[:, None], *(array[None, None] for array in own))


def solution(mesh):
    slots = P("owner", "dp", None, None)
    return jax.shard_map(
        body,
        mesh=mesh,
        in_specs=(P("dp", "owner", None, None), P(), P(), slots, slots, slots, slots),
        out_specs=(P(None, "dp", None, None), slots, slots, slots, slots),
        check_vma=False,
    )
```
